128 devices in a mesh: fsdp: 16 (over x, z), ctx: 8 (over y, core).
Axes of the slice: x: 4, y: 4, z: 4, core: 2. Of those that a mesh axis runs over, the one named last changes fastest.
Arguments:
- tokens: bfloat16 [16, 1024, 4096], P('fsdp', 'ctx'), may hold values from -6 to 6
- norm_gain: float32 [4096], replicated, may hold values from 0.5 to 1.5
- w_in: bfloat16 [4096, 3, 4096], P(None, None, 'fsdp'), may hold values from -0.09375 to 0.09375
- taps: float32 [3, 3, 4096], P(None, None, 'fsdp'), may hold values from -3 to 3
- decay_rate: float32 [16, 4096], P(None, 'fsdp'), may hold values from 0 to 0.0334, as said below
- residues: float32 [16, 4096], P(None, 'fsdp'), may hold values from -0.12 to 0.12
- skip_gain: float32 [4096], P('fsdp'), may hold values from -4 to 4
- w_out: bfloat16 [4096, 4096], P('fsdp'), may hold values from -0.09375 to 0.09375
Outputs:
- mixed: bfloat16 [16, 1024, 4096], P('fsdp', 'ctx')
The draws below stay inside these ranges and needn't reach their ends.
Inputs may be any that keep to these rules, and one draw needn't show every extreme that they name: `decay_rate`: positive decay rates of the poles, at most 1/30.
All inputs are finite; a program needn't handle non-finite values.
Results may differ from the reference program's by a relative error of at most 0.024.
Values may be sent and summed in bfloat16 or wider, within the bound.
No kernel may reach another device: no remote copies, remote signals or barrier semaphores. Data moves between devices by JAX's collectives and lax.ppermute only.
A program may use at most 192 MiB of HBM per device.

```python
import math
import jax
import jax.numpy as jnp
from jax import lax

D = 4096
NP = 16
TAPS = 3
TOK_DEV = 128
SEQ = 1024
SEQS = 16
N_FSDP = 16
N_CTX = 8


def draw_decay_rate(key, part):
    key = jax.random.fold_in(key, 11)
    lower = math.log(0.3 / SEQ)
    upper = math.log(1.0 / 30.0)
    exponent = jax.random.uniform(key, (NP, D), jnp.float32, lower, upper)
    return jnp.exp(exponent)


def level_of(own_key, shape, cuts, least, largest):
    gain, own = 1.0, jax.random.fold_in(own_key, 6)
    for dim, shards_of in cuts:
        steps = jnp.exp(jax.random.uniform(jax.random.fold_in(own, dim), (shards_of,), jnp.float32, least / len(cuts), largest / len(cuts)))
        gain = gain * jnp.repeat(steps, shape[dim] // shards_of).reshape([-1 if axis == dim else 1 for axis in range(len(shape))])
    return gain


def bell_draw(stream_key, shape, spread, bound, pieces=(), held_as=jnp.bfloat16):
    array = jax.random.normal(stream_key, shape, jnp.float32) * spread
    if len(pieces) > 0:
        array = level_of(stream_key, shape, pieces, -0.22, 0.18) * array
    return jnp.clip(array, min=-bound, max=bound).astype(held_as)


def setup_inputs(seed: int = 0) -> dict:
    key_of = jax.random.split(jax.random.key(seed), 9)
    return {
        "tokens": bell_draw(key_of[0], (SEQS, SEQ, D), 1.0, 6.0, ((0, 16), (1, 8))),
        "norm_gain": jnp.clip(1.0 + 0.1 * jax.random.normal(key_of[1], (D,), jnp.float32), 0.5, 1.5),
        "w_in": bell_draw(key_of[2], (D, 3, D), D ** -0.5, 0.09375, ((2, 16),)),
        "taps": bell_draw(key_of[3], (TAPS, 3, D), 0.6, 3.0, ((2, 16),), jnp.float32),
        "decay_rate": draw_decay_rate(jax.random.fold_in(key_of[8], 71), 0),
        "residues": bell_draw(key_of[5], (NP, D), 0.02, 0.12, ((1, 16),), jnp.float32),
        "skip_gain": bell_draw(key_of[6], (D,), 1.0, 4.0, ((0, 16),), jnp.float32),
        "w_out": bell_draw(key_of[7], (D, D), D ** -0.5, 0.09375, ((0, 16),)),
    }


def reference(tokens, norm_gain, w_in, taps, decay_rate, residues, skip_gain, w_out):
    high = lax.Precision.HIGHEST
    values = tokens.astype(jnp.float32)
    inverse_rms = lax.rsqrt(lax.optimization_barrier(jnp.mean(values * values, axis=-1, keepdims=True)) + 1e-06)
    normed = (values * inverse_rms * norm_gain).astype(jnp.bfloat16)
    features = jnp.dot(normed.reshape(SEQS * SEQ, D), w_in.reshape(D, 3 * D), preferred_element_type=jnp.float32)
    features = features.astype(jnp.bfloat16).reshape(SEQS, SEQ, 3, D).astype(jnp.float32)
    padded = jnp.pad(features, ((0, 0), (2, 0), (0, 0), (0, 0)))
    filtered = taps[0] * padded[:, 2:] + taps[1] * padded[:, 1:-1] + taps[2] * padded[:, :-2]
    query_part = filtered[:, :, 0]
    product = filtered[:, :, 1] * filtered[:, :, 2]
    offsets = jnp.arange(TOK_DEV, dtype=jnp.float32)
    powers = jnp.exp(-decay_rate[:, None, :] * offsets[None, :, None])
    kernel = lax.optimization_barrier(jnp.sum(residues[:, None, :] * powers, axis=0))
    positions = jnp.arange(TOK_DEV, dtype=jnp.int32)
    lag_steps = positions[:, None] - positions[None, :]
    toeplitz = jnp.where((lag_steps >= 0)[:, :, None], kernel[jnp.maximum(lag_steps, 0)], jnp.float32(0.0))
    end_pow = jnp.exp(-decay_rate[:, None, :] * (TOK_DEV - 1 - offsets)[None, :, None])
    enter = residues[:, None, :] * jnp.exp(-decay_rate[:, None, :] * (offsets + 1.0)[None, :, None])
    decay_all = jnp.exp(-decay_rate * TOK_DEV)
    blocks = product.reshape(SEQS, N_CTX, TOK_DEV, D).transpose(1, 0, 2, 3)

    def advance(carried, block_rows):
        inside = jnp.einsum('tsc,gsc->gtc', toeplitz, block_rows, precision=high)
        entering = jnp.einsum('ntc,gnc->gtc', enter, carried, precision=high)
        summary = jnp.einsum('nsc,gsc->gnc', end_pow, block_rows, precision=high)
        return (decay_all * carried + summary, inside + entering)
    _, conv = lax.scan(advance, jnp.zeros((SEQS, NP, D), jnp.float32), blocks)
    conv = conv.transpose(1, 0, 2, 3).reshape(SEQS, SEQ, D)
    response = skip_gain * product + conv
    gated = (query_part * response).astype(jnp.bfloat16)
    flat_rows = gated.reshape(SEQS * SEQ, D)
    block_width = D // N_FSDP

    def add_part(running, which):
        first = (which * block_width).astype(jnp.int32)
        columns = lax.dynamic_slice_in_dim(flat_rows, first, block_width, 1)
        weights = lax.dynamic_slice_in_dim(w_out, first, block_width, 0)
        partial_value = jnp.dot(columns, weights, preferred_element_type=jnp.float32).astype(jnp.bfloat16)
        partial_value = lax.optimization_barrier(partial_value)
        return (running + partial_value.astype(jnp.float32), None)
    running, _ = lax.scan(add_part, jnp.zeros((SEQS * SEQ, D), jnp.float32), jnp.arange(N_FSDP, dtype=jnp.int32))
    result = values.reshape(SEQS * SEQ, D) + running
    return result.astype(jnp.bfloat16).reshape(SEQS, SEQ, D)
```

```python
import jax
import jax.numpy as jnp
from jax import lax
from jax.experimental import pallas as pl
from jax.experimental.pallas import tpu as pltpu
from jax.sharding import Mesh, PartitionSpec as P

F32 = jnp.float32
BF16 = jnp.bfloat16
OFFSETS = (0, 1, 3, 2)
CHUNK = 16
EDGE = 8


def from_ahead(value, axis, steps):
    count = lax.axis_size(axis)
    return lax.ppermute(value, axis, [(i, (i - steps) % count) for i in range(count)])


def from_behind(value, axis, steps):
    count = lax.axis_size(axis)
    return lax.ppermute(value, axis, [(i, i + steps) for i in range(count - steps)])


def compiler_params():
    return pltpu.CompilerParams(vmem_limit_bytes=44 * 1024 * 1024)


def project(x_ref, w_ref, scratch, seqs, length):
    pieces, depth, width = w_ref.shape
    total = jnp.dot(x_ref[:, :depth], w_ref[0], preferred_element_type=F32)
    for k in range(1, pieces):
        total += jnp.dot(x_ref[:, k * depth : (k + 1) * depth], w_ref[k], preferred_element_type=F32)
    total = total.astype(BF16).astype(F32)
    rows = seqs * length
    for lane in range(width // 128):
        cols = slice(lane * 128, (lane + 1) * 128)
        for s in range(seqs):
            scratch[lane, s, EDGE : EDGE + length, :] = total[s * length : (s + 1) * length, cols]
            scratch[lane, s, EDGE - 2 : EDGE, :] = total[rows + 2 * s : rows + 2 * s + 2, cols]


def wide(row):
    return jnp.broadcast_to(row, (8, 128))


def kv_kernel(order, x_ref, w_ref, taps_ref, kern_ref, pole_ref, jump_ref, y_ref, e_ref, t_ref, fk, fv):
    seqs = fk.shape[1]
    length = fk.shape[2] - EDGE
    project(x_ref, w_ref.at[0, :, 0], fk, seqs, length)
    project(x_ref, w_ref.at[0, :, 1], fv, seqs, length)
    first_row = lax.broadcasted_iota(jnp.int32, (8, 128), 0)

    def each(i, carry):
        lane, s = i // seqs, i % seqs
        tap = lambda j, stream: wide(taps_ref[0, lane, pl.ds(3 * j + stream, 1), :])
        kt = [tap(j, 1) for j in range(3)]
        vt = [tap(j, 2) for j in range(3)]
        kx = [fk[lane, s, pl.ds(EDGE + t, 8, stride=CHUNK), :] for t in range(-2, CHUNK)]
        vx = [fv[lane, s, pl.ds(EDGE + t, 8, stride=CHUNK), :] for t in range(-2, CHUNK)]
        xs = []
        for t in range(CHUNK):
            k = kt[0] * kx[t + 2] + kt[1] * kx[t + 1] + kt[2] * kx[t]
            v = vt[0] * vx[t + 2] + vt[1] * vx[t + 1] + vt[2] * vx[t]
            xs.append(k * v)
        kern = [wide(kern_ref[0, lane, pl.ds(d, 1), :]) for d in range(CHUNK)]
        for t in range(CHUNK):
            y = kern[0] * xs[t]
            for d in range(1, t + 1):
                y += kern[d] * xs[t - d]
            y_ref[0, lane, s, t] = y
        for n in range(16):
            pole = wide(pole_ref[0, lane, pl.ds(n, 1), :])
            state = xs[0]
            for t in range(1, CHUNK):
                state = pole * state + xs[t]
            for j, step in enumerate((1, 2, 4)):
                jump = wide(jump_ref[0, lane, j, pl.ds(n, 1), :])
                moved = jnp.where(first_row >= step, pltpu.roll(state, step, 0), 0.0)
                state = state + jump * moved
            e_ref[0, lane, s, n] = jnp.where(first_row >= 1, pltpu.roll(state, 1, 0), 0.0)
            t_ref[0, lane, s, pl.ds(n, 1), :] = state[7:8, :]
        return carry

    lax.fori_loop(0, seqs * fk.shape[0], each, 0)


def enter_kernel(y_ref, e_ref, in_ref, pole_ref, res_ref, ahead_ref, out_ref):
    lanes, seqs = y_ref.shape[1], y_ref.shape[2]

    def each(i, carry):
        lane, s = i // seqs, i % seqs
        poles, states = [], []
        for n in range(16):
            pole = wide(pole_ref[0, lane, pl.ds(n, 1), :])
            incoming = wide(in_ref[0, lane, s, pl.ds(n, 1), :])
            state = e_ref[0, lane, s, n] + ahead_ref[0, lane, n] * incoming
            poles.append(pole)
            states.append(wide(res_ref[0, lane, pl.ds(n, 1), :]) * pole * state)
        for t in range(CHUNK):
            total = y_ref[0, lane, s, t]
            for n in range(16):
                total += states[n]
            out_ref[0, lane, s, t] = total
            states = [pole * state for pole, state in zip(poles, states)]
        return carry

    lax.fori_loop(0, seqs * lanes, each, 0)


def q_kernel(order, x_ref, w_ref, taps_ref, y_ref, out_ref, fq, gated):
    lanes, seqs = fq.shape[:2]
    length = fq.shape[2] - EDGE
    project(x_ref, w_ref.at[0], fq, seqs, length)

    def each(i, carry):
        lane, s = i // seqs, i % seqs
        qt = [wide(taps_ref[0, lane, pl.ds(3 * j, 1), :]) for j in range(3)]
        qx = [fq[lane, s, pl.ds(EDGE + t, 8, stride=CHUNK), :] for t in range(-2, CHUNK)]
        for t in range(CHUNK):
            q = qt[0] * qx[t + 2] + qt[1] * qx[t + 1] + qt[2] * qx[t]
            gated[lane, s, pl.ds(t, 8, stride=CHUNK), :] = q * y_ref[0, lane, s, t]
        return carry

    lax.fori_loop(0, seqs * lanes, each, 0)
    for lane in range(lanes):
        for s in range(seqs):
            out_ref[0, s, :, lane * 128 : (lane + 1) * 128] = gated[lane, s].astype(BF16)


def out_kernel(order, g_ref, w_ref, *out_refs):
    blocks, seqs = g_ref.shape[:2]
    for s in range(seqs):
        total = jnp.dot(g_ref[0, s], w_ref[order[0]], preferred_element_type=F32)
        for r in range(1, blocks):
            total += jnp.dot(g_ref[r, s], w_ref[order[r]], preferred_element_type=F32)
        out_refs[s][...] = total.astype(BF16)


def shards(tokens, norm_gain, w_in, taps, decay_rate, residues, skip_gain, w_out):
    z = lax.axis_index("z")
    part = lax.axis_index("y") * 2 + lax.axis_index("c")
    order = jnp.stack([(z + step) % 4 for step in OFFSETS]).astype(jnp.int32)
    width, _, channels = w_in.shape
    length = tokens.shape[1]
    blocks = seqs = len(OFFSETS)
    lanes = channels // 128

    with jax.named_scope("weights"):
        w_streams = w_in.transpose(1, 0, 2)
        depth = width // 8
        kv_share = lax.dynamic_slice(w_streams, (1, part * depth, 0), (2, depth, channels))
        q_share = lax.dynamic_slice(w_streams, (0, part * depth, 0), (1, depth, channels))[0]
        out_share = lax.dynamic_slice(w_out, (part * (channels // 8), 0), (channels // 8, width))
        plane = ("z", "y", "c")
        w_kv = lax.all_gather(kv_share, plane, axis=0).reshape(blocks, 8, 2, depth, channels)
        q_share, w_kv = lax.optimization_barrier((q_share, w_kv))
        w_q = lax.all_gather(q_share, plane, axis=0).reshape(blocks, 8, depth, channels)
        out_share, w_q = lax.optimization_barrier((out_share, w_q))
        w_o = lax.all_gather(out_share, plane, axis=0).reshape(blocks, channels, width)

    with jax.named_scope("norm"):
        values = tokens[0].astype(F32)
        inverse_rms = lax.rsqrt(jnp.mean(values * values, axis=-1, keepdims=True) + 1e-06)
        normed = (values * inverse_rms * norm_gain).astype(BF16)

    with jax.named_scope("gather_tokens"):
        last = normed[length - 2 :]
        edges = []
        for step in OFFSETS:
            pairs = [
                (((x * 4 + y) * 2 + c), (((x - step) % 4 * 4) + (y * 2 + c + 1) // 2) * 2 + (c + 1) % 2)
                for x in range(4)
                for y in range(4)
                for c in range(2)
                if y * 2 + c < 7
            ]
            edges.append(lax.ppermute(last, ("x", "y", "c"), pairs))
        rows = [normed] + [from_ahead(normed, "x", step) for step in OFFSETS[1:]]
        tail = jnp.zeros((16 - 2 * seqs, width), BF16)
        x_all = jnp.concatenate(rows + edges + [tail], axis=0)

    with jax.named_scope("params"):
        packed = jnp.concatenate(
            [taps.reshape(9, channels), decay_rate, residues, skip_gain[None], jnp.zeros((6, channels), F32)], axis=0
        )
        packed = jnp.stack([packed] + [from_ahead(packed, "z", step) for step in OFFSETS[1:]])
        packed = packed.reshape(blocks, 48, lanes, 128).transpose(0, 2, 1, 3)
        taps_all, decay, res = packed[:, :, :9], packed[:, :, 9:25], packed[:, :, 25:41]
        lags = jnp.arange(CHUNK, dtype=F32)
        kern = jnp.sum(res[:, :, None] * jnp.exp(-decay[:, :, None] * lags[:, None, None]), axis=3)
        kern = kern.at[:, :, 0].add(packed[:, :, 41])
        pole = jnp.exp(-decay)
        jumps = jnp.exp(-decay[:, :, None] * jnp.array([CHUNK, 2 * CHUNK, 4 * CHUNK], F32)[:, None, None])
        ahead = jnp.exp(-decay[:, :, :, None] * (CHUNK * jnp.arange(8, dtype=F32))[:, None])

    def blocked(shape, index=None):
        index = index or (lambda r, order: (r,))
        return pl.BlockSpec((1,) + shape, lambda r, *o: index(r, *o) + (0,) * len(shape))

    whole_x = pl.BlockSpec(x_all.shape, lambda r, *o: (0, 0))
    by_order = lambda r, order: (order[r],)
    same = lambda r, *o: (r,)
    scratch = pltpu.VMEM((lanes, seqs, EDGE + length, 128), F32)
    by_chunk = (lanes, seqs, CHUNK, 8, 128)
    with jax.named_scope("keys_values"):
        y, e, ends = pl.pallas_call(
            kv_kernel,
            grid_spec=pltpu.PrefetchScalarGridSpec(
                num_scalar_prefetch=1,
                grid=(blocks,),
                in_specs=[
                    whole_x,
                    blocked(w_kv.shape[1:], by_order),
                    blocked(taps_all.shape[1:], same),
                    blocked(kern.shape[1:], same),
                    blocked(pole.shape[1:], same),
                    blocked(jumps.shape[1:], same),
                ],
                out_specs=[blocked(by_chunk, same), blocked(by_chunk, same), blocked((lanes, seqs, 16, 128), same)],
                scratch_shapes=[scratch, scratch],
            ),
            out_shape=[
                jax.ShapeDtypeStruct((blocks,) + by_chunk, F32),
                jax.ShapeDtypeStruct((blocks,) + by_chunk, F32),
                jax.ShapeDtypeStruct((blocks, lanes, seqs, 16, 128), F32),
            ],
            compiler_params=compiler_params(),
            name="keys_values",
        )(order, x_all, w_kv, taps_all, kern, pole, jumps)

    with jax.named_scope("states"):
        core = lax.axis_index("c")
        span = jnp.exp(-decay * length)[:, :, None]
        sent = ends.astype(BF16)
        other = lax.ppermute(sent, "c", [(0, 1), (1, 0)]).astype(F32)
        sent = sent.astype(F32)
        front, back = jnp.where(core == 0, sent, other), jnp.where(core == 0, other, sent)
        chip = (span * front + back).astype(BF16)
        hops = [from_behind(chip, "y", step).astype(F32) for step in (1, 2, 3)]
        square = span * span
        incoming = hops[0] + square * (hops[1] + square * hops[2])
        incoming = jnp.where(core == 0, incoming, span * incoming + front)

    with jax.named_scope("entering"):
        response = pl.pallas_call(
            enter_kernel,
            grid=(blocks,),
            in_specs=[
                blocked(by_chunk, same),
                blocked(by_chunk, same),
                blocked(incoming.shape[1:], same),
                blocked(pole.shape[1:], same),
                blocked(res.shape[1:], same),
                blocked(ahead.shape[1:], same),
            ],
            out_specs=blocked(by_chunk, same),
            out_shape=jax.ShapeDtypeStruct((blocks,) + by_chunk, F32),
            compiler_params=compiler_params(),
            name="entering",
        )(y, e, incoming, pole, res, ahead)

    with jax.named_scope("query_gate"):
        gated = pl.pallas_call(
            q_kernel,
            grid_spec=pltpu.PrefetchScalarGridSpec(
                num_scalar_prefetch=1,
                grid=(blocks,),
                in_specs=[
                    whole_x,
                    blocked(w_q.shape[1:], by_order),
                    blocked(taps_all.shape[1:], same),
                    blocked(by_chunk, same),
                ],
                out_specs=blocked((seqs, length, channels), same),
                scratch_shapes=[scratch, pltpu.VMEM((lanes, seqs, length, 128), F32)],
            ),
            out_shape=jax.ShapeDtypeStruct((blocks, seqs, length, channels), BF16),
            compiler_params=compiler_params(),
            name="query_gate",
        )(order, x_all, w_q, taps_all, response)

    with jax.named_scope("project_out"):
        cols = 512
        partial = pl.pallas_call(
            out_kernel,
            grid_spec=pltpu.PrefetchScalarGridSpec(
                num_scalar_prefetch=1,
                grid=(width // cols,),
                in_specs=[
                    pl.BlockSpec(gated.shape, lambda i, order: (0, 0, 0, 0)),
                    pl.BlockSpec((blocks, channels, cols), lambda i, order: (0, 0, i)),
                ],
                out_specs=[pl.BlockSpec((length, cols), lambda i, order: (0, i))] * seqs,
            ),
            out_shape=[jax.ShapeDtypeStruct((length, width), BF16)] * seqs,
            compiler_params=compiler_params(),
            name="project_out",
        )(order, gated, w_o)

    with jax.named_scope("sum_parts"):
        total = values + partial[0].astype(F32)
        for s, step in enumerate(OFFSETS):
            if step:
                total += from_ahead(partial[s], "x", -step).astype(F32)
        return total.astype(BF16)[None]


def solution(mesh):
    fine = Mesh(mesh.devices.reshape(4, 4, 4, 2), ("x", "z", "y", "c"))
    fsdp, ctx = ("x", "z"), ("y", "c")
    in_specs = (
        P(fsdp, ctx, None),
        P(),
        P(None, None, fsdp),
        P(None, None, fsdp),
        P(None, fsdp),
        P(None, fsdp),
        P(fsdp),
        P(fsdp, None),
    )
    return jax.shard_map(shards, mesh=fine, in_specs=in_specs, out_specs=P(fsdp, ctx, None), check_vma=False)
```

```python
import jax
import jax.numpy as jnp
from jax import lax
from jax.experimental import pallas as pl
from jax.experimental.pallas import tpu as pltpu
from jax.sharding import Mesh, PartitionSpec as P

F32 = jnp.float32
BF16 = jnp.bfloat16
OFFSETS = (0, 1, 3, 2)
CHUNK = 16
EDGE = 8


def from_ahead(value, axis, steps):
    count = lax.axis_size(axis)
    return lax.ppermute(value, axis, [(i, (i - steps) % count) for i in range(count)])


def from_behind(value, axis, steps):
    count = lax.axis_size(axis)
    return lax.ppermute(value, axis, [(i, i + steps) for i in range(count - steps)])


def compiler_params():
    return pltpu.CompilerParams(vmem_limit_bytes=44 * 1024 * 1024)


def load_rows(row_refs, x, sems):
    copies, first = [], 0
    for i, ref in enumerate(row_refs):
        copies.append(pltpu.make_async_copy(ref, x.at[pl.ds(first, ref.shape[0])], sems.at[i]))
        first += ref.shape[0]
    for copy in copies:
        copy.start()
    for copy in copies:
        copy.wait()


def dot(a, b):
    return jnp.dot(a, b, preferred_element_type=F32)


def from_pieces(quarter, x, own_ref, piece_refs, out):
    depth = piece_refs[0].shape[1]
    block = pl.program_id(0)

    @pl.when(block == 0)
    def _():
        out[...] = dot(x[...], own_ref[...])

    @pl.when(block > 0)
    def _():
        total = None
        for i, ref in enumerate(piece_refs):
            part = dot(x[:, pl.ds(pl.multiple_of(quarter[i] * depth, depth), depth)], ref[0])
            total = part if total is None else total + part
        out[...] = total


def lay_out(total, scratch, seqs, length):
    rows = seqs * length
    for lane in range(scratch.shape[0]):
        cols = slice(lane * 128, (lane + 1) * 128)
        for s in range(seqs):
            scratch[lane, s, EDGE : EDGE + length, :] = total[s * length : (s + 1) * length, cols]
            scratch[lane, s, EDGE - 2 : EDGE, :] = total[rows + 2 * s : rows + 2 * s + 2, cols]


def k_kernel(quarter, own_ref, p0, p1, p2, p3, r0, r1, r2, r3, r4, out_ref, x, total, sems):
    @pl.when(pl.program_id(0) == 0)
    def _():
        load_rows((r0, r1, r2, r3, r4), x, sems)

    from_pieces(quarter, x, own_ref, (p0, p1, p2, p3), total)
    out_ref[0] = total[...].astype(BF16)


def wide(row):
    return jnp.broadcast_to(row, (8, 128))


def v_kernel(
    quarter, own_ref, p0, p1, p2, p3, r0, r1, r2, r3, r4, k_ref, taps_ref, kern_ref, pole_ref, jump_ref,
    y_ref, e_ref, t_ref, x, total, sems, fk, fv,
):
    seqs = fk.shape[1]
    length = fk.shape[2] - EDGE

    @pl.when(pl.program_id(0) == 0)
    def _():
        load_rows((r0, r1, r2, r3, r4), x, sems)

    from_pieces(quarter, x, own_ref, (p0, p1, p2, p3), total)
    lay_out(k_ref[0].astype(F32), fk, seqs, length)
    lay_out(total[...].astype(BF16).astype(F32), fv, seqs, length)
    first_row = lax.broadcasted_iota(jnp.int32, (8, 128), 0)

    def each(i, carry):
        lane, s = i // seqs, i % seqs
        tap = lambda j, stream: wide(taps_ref[0, lane, pl.ds(3 * j + stream, 1), :])
        kt = [tap(j, 1) for j in range(3)]
        vt = [tap(j, 2) for j in range(3)]
        kx = [fk[lane, s, pl.ds(EDGE + t, 8, stride=CHUNK), :] for t in range(-2, CHUNK)]
        vx = [fv[lane, s, pl.ds(EDGE + t, 8, stride=CHUNK), :] for t in range(-2, CHUNK)]
        xs = []
        for t in range(CHUNK):
            k = kt[0] * kx[t + 2] + kt[1] * kx[t + 1] + kt[2] * kx[t]
            v = vt[0] * vx[t + 2] + vt[1] * vx[t + 1] + vt[2] * vx[t]
            xs.append(k * v)
        kern = [wide(kern_ref[0, lane, pl.ds(d, 1), :]) for d in range(CHUNK)]
        for t in range(CHUNK):
            y = kern[0] * xs[t]
            for d in range(1, t + 1):
                y += kern[d] * xs[t - d]
            y_ref[0, lane, s, t] = y
        for n in range(16):
            pole = wide(pole_ref[0, lane, pl.ds(n, 1), :])
            state = xs[0]
            for t in range(1, CHUNK):
                state = pole * state + xs[t]
            for j, step in enumerate((1, 2, 4)):
                jump = wide(jump_ref[0, lane, j, pl.ds(n, 1), :])
                moved = jnp.where(first_row >= step, pltpu.roll(state, step, 0), 0.0)
                state = state + jump * moved
            e_ref[0, lane, s, n] = jnp.where(first_row >= 1, pltpu.roll(state, 1, 0), 0.0)
            t_ref[0, lane, s, pl.ds(n, 1), :] = state[7:8, :]
        return carry

    lax.fori_loop(0, seqs * fk.shape[0], each, 0)


def enter_kernel(y_ref, e_ref, in_ref, pole_ref, res_ref, ahead_ref, out_ref):
    lanes, seqs = y_ref.shape[1], y_ref.shape[2]

    def each(i, carry):
        lane, s = i // seqs, i % seqs
        poles, states = [], []
        for n in range(16):
            pole = wide(pole_ref[0, lane, pl.ds(n, 1), :])
            incoming = wide(in_ref[0, lane, s, pl.ds(n, 1), :])
            state = e_ref[0, lane, s, n] + ahead_ref[0, lane, n] * incoming
            poles.append(pole)
            states.append(wide(res_ref[0, lane, pl.ds(n, 1), :]) * pole * state)
        for t in range(CHUNK):
            total = y_ref[0, lane, s, t]
            for n in range(16):
                total += states[n]
            out_ref[0, lane, s, t] = total
            states = [pole * state for pole, state in zip(poles, states)]
        return carry

    lax.fori_loop(0, seqs * lanes, each, 0)


def q_kernel(order, w_ref, r0, r1, r2, r3, r4, taps_ref, y_ref, out_ref, x, sems, fq, gated):
    lanes, seqs = fq.shape[:2]
    length = fq.shape[2] - EDGE
    _, pieces, depth, _ = w_ref.shape

    @pl.when(pl.program_id(0) == 0)
    def _():
        load_rows((r0, r1, r2, r3, r4), x, sems)

    total = dot(x[:, :depth], w_ref[0, 0])
    for k in range(1, pieces):
        total += dot(x[:, k * depth : (k + 1) * depth], w_ref[0, k])
    lay_out(total.astype(BF16).astype(F32), fq, seqs, length)

    def each(i, carry):
        lane, s = i // seqs, i % seqs
        qt = [wide(taps_ref[0, lane, pl.ds(3 * j, 1), :]) for j in range(3)]
        qx = [fq[lane, s, pl.ds(EDGE + t, 8, stride=CHUNK), :] for t in range(-2, CHUNK)]
        for t in range(CHUNK):
            q = qt[0] * qx[t + 2] + qt[1] * qx[t + 1] + qt[2] * qx[t]
            gated[lane, s, pl.ds(t, 8, stride=CHUNK), :] = q * y_ref[0, lane, s, t]
        return carry

    lax.fori_loop(0, seqs * lanes, each, 0)
    for lane in range(lanes):
        for s in range(seqs):
            out_ref[0, s, :, lane * 128 : (lane + 1) * 128] = gated[lane, s].astype(BF16)


def out_kernel(order, g_ref, w_ref, *out_refs):
    blocks, seqs, length, channels = g_ref.shape
    total = [None] * 2
    for r in range(blocks):
        rows = g_ref[r].reshape(seqs * length, channels)
        for half in range(2):
            part = dot(rows, w_ref[order[r], 0, half * channels : (half + 1) * channels, :])
            total[half] = part if r == 0 else total[half] + part
    for s in range(seqs):
        for half in range(2):
            out_refs[s][:, half * 256 : (half + 1) * 256] = total[half][s * length : (s + 1) * length].astype(BF16)


def shards(tokens, norm_gain, w_in, taps, decay_rate, residues, skip_gain, w_out):
    z = lax.axis_index("z")
    part = lax.axis_index("y") * 2 + lax.axis_index("c")
    order = jnp.stack([(z + step) % 4 for step in OFFSETS]).astype(jnp.int32)
    width, _, channels = w_in.shape
    length = tokens.shape[1]
    blocks = seqs = len(OFFSETS)
    lanes = channels // 128

    with jax.named_scope("background_weights"):
        w_streams = w_in.transpose(1, 0, 2)
        depth = width // 8
        q_share = lax.dynamic_slice(w_streams, (0, part * depth, 0), (1, depth, channels))[0]
        out_share = [lax.dynamic_slice(w_out, (0, part * depth + half * 256), (channels, 256)) for half in range(2)]
        w_qo = lax.all_gather(jnp.concatenate([q_share] + out_share, axis=0), ("z", "y", "c"), axis=0)
        w_qo = w_qo.reshape(blocks, 8, 2 * depth, channels)

    with jax.named_scope("norm"):
        values = tokens[0].astype(F32)
        inverse_rms = lax.rsqrt(jnp.mean(values * values, axis=-1, keepdims=True) + 1e-06)
        normed = (values * inverse_rms * norm_gain).astype(BF16)

    with jax.named_scope("gather_tokens"):
        last = normed[length - 2 :]
        edges = []
        for step in OFFSETS:
            pairs = [
                (((x * 4 + y) * 2 + c), (((x - step) % 4 * 4) + (y * 2 + c + 1) // 2) * 2 + (c + 1) % 2)
                for x in range(4)
                for y in range(4)
                for c in range(2)
                if y * 2 + c < 7
            ]
            edges.append(lax.ppermute(last, ("x", "y", "c"), pairs))
        rows = [normed] + [from_ahead(normed, "x", step) for step in OFFSETS[1:]]
        rows.append(jnp.concatenate(edges + [jnp.zeros((16 - 2 * seqs, width), BF16)], axis=0))

    with jax.named_scope("gather_kv_weights"):
        parity, core = lax.axis_index("y") % 2, lax.axis_index("c")
        own_quarter = 2 * parity + core
        quarter = jnp.stack([own_quarter, own_quarter ^ 2, own_quarter ^ 1, own_quarter ^ 3]).astype(jnp.int32)
        pieces = []
        for stream, way in ((1, 1), (2, -1)):
            share = lax.dynamic_slice(w_streams, (stream, own_quarter * (width // 4), 0), (1, width // 4, channels))[0]
            ahead = from_ahead(share, "z", 1)
            behind = from_ahead(share, "z", -1)
            far = from_ahead(behind if way == 1 else ahead, "z", -way)
            along_z = jnp.stack([ahead, behind, far])
            along_y = jnp.stack([from_ahead(ahead, "y", 1), from_ahead(behind, "y", -1), from_ahead(far, "y", -way)])
            pieces.append([along_z, along_y, from_ahead(along_z, "c", 1), from_ahead(along_y, "c", 1)])

    with jax.named_scope("params"):
        packed = jnp.concatenate(
            [taps.reshape(9, channels), decay_rate, residues, skip_gain[None], jnp.zeros((6, channels), F32)], axis=0
        )
        packed = jnp.stack([packed] + [from_ahead(packed, "z", step) for step in OFFSETS[1:]])
        packed = packed.reshape(blocks, 48, lanes, 128).transpose(0, 2, 1, 3)
        taps_all, decay, res = packed[:, :, :9], packed[:, :, 9:25], packed[:, :, 25:41]
        lags = jnp.arange(CHUNK, dtype=F32)
        kern = jnp.sum(res[:, :, None] * jnp.exp(-decay[:, :, None] * lags[:, None, None]), axis=3)
        kern = kern.at[:, :, 0].add(packed[:, :, 41])
        pole = jnp.exp(-decay)
        jumps = jnp.exp(-decay[:, :, None] * jnp.array([CHUNK, 2 * CHUNK, 4 * CHUNK], F32)[:, None, None])
        ahead = jnp.exp(-decay[:, :, :, None] * (CHUNK * jnp.arange(8, dtype=F32))[:, None])

    def blocked(shape, index=None):
        index = index or (lambda r, order: (r,))
        return pl.BlockSpec((1,) + shape, lambda r, *o: index(r, *o) + (0,) * len(shape))

    by_order = lambda r, order: (order[r],)
    same = lambda r, *o: (r,)
    scratch = pltpu.VMEM((lanes, seqs, EDGE + length, 128), F32)
    by_chunk = (lanes, seqs, CHUNK, 8, 128)
    high = seqs * length + 16
    in_place = [pl.BlockSpec(memory_space=pl.ANY)] * len(rows)
    x_scratch, row_sems = pltpu.VMEM((high, width), BF16), pltpu.SemaphoreType.DMA((len(rows),))
    weight_specs = [pl.BlockSpec((width, channels), lambda r, *o: (0, 0))]
    weight_specs += [blocked((width // 4, channels), lambda r, *o: (jnp.maximum(r - 1, 0),))] * 4
    with jax.named_scope("keys"):
        keys = pl.pallas_call(
            k_kernel,
            grid_spec=pltpu.PrefetchScalarGridSpec(
                num_scalar_prefetch=1,
                grid=(blocks,),
                in_specs=weight_specs + in_place,
                out_specs=blocked((high, channels), same),
                scratch_shapes=[x_scratch, pltpu.VMEM((high, channels), F32), row_sems],
            ),
            out_shape=jax.ShapeDtypeStruct((blocks, high, channels), BF16),
            compiler_params=compiler_params(),
            name="keys",
        )(quarter, w_streams[1], *pieces[0], *rows)
    with jax.named_scope("values_filter"):
        y, e, ends = pl.pallas_call(
            v_kernel,
            grid_spec=pltpu.PrefetchScalarGridSpec(
                num_scalar_prefetch=1,
                grid=(blocks,),
                in_specs=weight_specs
                + in_place
                + [
                    blocked((high, channels), same),
                    blocked(taps_all.shape[1:], same),
                    blocked(kern.shape[1:], same),
                    blocked(pole.shape[1:], same),
                    blocked(jumps.shape[1:], same),
                ],
                out_specs=[blocked(by_chunk, same), blocked(by_chunk, same), blocked((lanes, seqs, 16, 128), same)],
                scratch_shapes=[x_scratch, pltpu.VMEM((high, channels), F32), row_sems, scratch, scratch],
            ),
            out_shape=[
                jax.ShapeDtypeStruct((blocks,) + by_chunk, F32),
                jax.ShapeDtypeStruct((blocks,) + by_chunk, F32),
                jax.ShapeDtypeStruct((blocks, lanes, seqs, 16, 128), F32),
            ],
            compiler_params=compiler_params(),
            name="values_filter",
        )(quarter, w_streams[2], *pieces[1], *rows, keys, taps_all, kern, pole, jumps)

    with jax.named_scope("states"):
        span = jnp.exp(-decay * length)[:, :, None]
        sent = ends.astype(BF16)
        other = lax.ppermute(sent, "c", [(0, 1), (1, 0)]).astype(F32)
        sent = sent.astype(F32)
        front, back = jnp.where(core == 0, sent, other), jnp.where(core == 0, other, sent)
        chip = (span * front + back).astype(BF16)
        hops = [from_behind(chip, "y", step).astype(F32) for step in (1, 2, 3)]
        square = span * span
        incoming = hops[0] + square * (hops[1] + square * hops[2])
        incoming = jnp.where(core == 0, incoming, span * incoming + front)

    with jax.named_scope("entering"):
        response = pl.pallas_call(
            enter_kernel,
            grid=(blocks,),
            in_specs=[
                blocked(by_chunk, same),
                blocked(by_chunk, same),
                blocked(incoming.shape[1:], same),
                blocked(pole.shape[1:], same),
                blocked(res.shape[1:], same),
                blocked(ahead.shape[1:], same),
            ],
            out_specs=blocked(by_chunk, same),
            out_shape=jax.ShapeDtypeStruct((blocks,) + by_chunk, F32),
            compiler_params=compiler_params(),
            name="entering",
        )(y, e, incoming, pole, res, ahead)

    with jax.named_scope("query_gate"):
        gated = pl.pallas_call(
            q_kernel,
            grid_spec=pltpu.PrefetchScalarGridSpec(
                num_scalar_prefetch=1,
                grid=(blocks,),
                in_specs=[blocked((8, depth, channels), by_order)]
                + in_place
                + [blocked(taps_all.shape[1:], same), blocked(by_chunk, same)],
                out_specs=blocked((seqs, length, channels), same),
                scratch_shapes=[x_scratch, row_sems, scratch, pltpu.VMEM((lanes, seqs, length, 128), F32)],
            ),
            out_shape=jax.ShapeDtypeStruct((blocks, seqs, length, channels), BF16),
            compiler_params=compiler_params(),
            name="query_gate",
        )(order, w_qo, *rows, taps_all, response)

    with jax.named_scope("project_out"):
        cols = 512
        partial = pl.pallas_call(
            out_kernel,
            grid_spec=pltpu.PrefetchScalarGridSpec(
                num_scalar_prefetch=1,
                grid=(width // cols,),
                in_specs=[
                    pl.BlockSpec(gated.shape, lambda i, order: (0, 0, 0, 0)),
                    pl.BlockSpec((blocks, 1, depth, channels), lambda i, order: (0, i, 1, 0)),
                ],
                out_specs=[pl.BlockSpec((length, cols), lambda i, order: (0, i))] * seqs,
            ),
            out_shape=[jax.ShapeDtypeStruct((length, width), BF16)] * seqs,
            compiler_params=compiler_params(),
            name="project_out",
        )(order, gated, w_qo)

    with jax.named_scope("sum_parts"):
        total = values + partial[0].astype(F32)
        for s, step in enumerate(OFFSETS):
            if step:
                total += from_ahead(partial[s], "x", -step).astype(F32)
        return total.astype(BF16)[None]


def solution(mesh):
    fine = Mesh(mesh.devices.reshape(4, 4, 4, 2), ("x", "z", "y", "c"))
    fsdp, ctx = ("x", "z"), ("y", "c")
    in_specs = (
        P(fsdp, ctx, None),
        P(),
        P(None, None, fsdp),
        P(None, None, fsdp),
        P(None, fsdp),
        P(None, fsdp),
        P(fsdp),
        P(fsdp, None),
    )
    return jax.shard_map(shards, mesh=fine, in_specs=in_specs, out_specs=P(fsdp, ctx, None), check_vma=False)
```

```python
import functools

import jax
import jax.numpy as jnp
from jax import lax
from jax.experimental import pallas as pl
from jax.experimental.pallas import tpu as pltpu
from jax.sharding import Mesh, PartitionSpec as P

F32 = jnp.float32
BF16 = jnp.bfloat16
OFFSETS = (0, 1, 3, 2)
CHUNK = 16
HEAD = 16
QUERY, KEY, VALUE = 0, 1, 2


def from_ahead(value, axis, steps):
    count = lax.axis_size(axis)
    return lax.ppermute(value, axis, [(i, (i - steps) % count) for i in range(count)])


def from_behind(value, axis, steps):
    count = lax.axis_size(axis)
    return lax.ppermute(value, axis, [(i, i + steps) for i in range(count - steps)])


def gather_along(value, axis):
    return [value] + [from_ahead(value, axis, step) for step in OFFSETS[1:]]


def compiler_params():
    return pltpu.CompilerParams(vmem_limit_bytes=60 * 1024 * 1024)


def norm_kernel(edge_ref, tokens_ref, gain_ref, out_ref, natural):
    def normed(rows):
        values = rows.astype(F32)
        inverse_rms = lax.rsqrt(jnp.mean(values * values, axis=-1, keepdims=True) + 1e-06)
        return values * inverse_rms * gain_ref[...]

    out_ref[:HEAD] = normed(edge_ref[...]).astype(BF16)
    values = normed(tokens_ref[0])
    for lane in range(natural.shape[0]):
        cols = slice(lane * 128, (lane + 1) * 128)
        natural[lane] = values[:, cols]
        for t in range(0, CHUNK, 2):
            pair = [natural[lane, pl.ds(t + i, 8, stride=CHUNK), :] for i in range(2)]
            out_ref[HEAD + 8 * t : HEAD + 8 * t + 16, cols] = jnp.concatenate(pair, axis=0).astype(BF16)


def pack_kernel(taps_ref, decay_ref, res_ref, skip_ref, out_ref):
    out_ref[...] = jnp.zeros_like(out_ref)
    for j in range(3):
        out_ref[3 * j : 3 * j + 3] = taps_ref[j]
    out_ref[16:32] = decay_ref[...]
    out_ref[32:48] = res_ref[...]
    out_ref[9:10] = skip_ref[...]


def coefficient_kernel(p0, p1, p2, p3, taps_ref, kern_ref, pole_ref, jump_ref, res_ref, reach_ref, span_ref):
    chunk_of = lax.broadcasted_iota(jnp.int32, (8, 128), 0).astype(F32) * CHUNK
    for r, packed in enumerate((p0, p1, p2, p3)):
        for lane in range(2):
            cols = slice(lane * 128, (lane + 1) * 128)
            decay, res = packed[16:32, cols], packed[32:48, cols]
            taps_ref[r, lane] = packed[0:16, cols]
            pole_ref[r, lane] = jnp.exp(-decay)
            res_ref[r, lane] = res
            span_ref[r, lane] = jnp.exp(-decay * (8 * CHUNK))
            for j in range(3):
                jump_ref[r, lane, j] = jnp.exp(-decay * (CHUNK << j))
            for d in range(CHUNK):
                row = jnp.sum(res * jnp.exp(-decay * d), axis=0, keepdims=True)
                kern_ref[r, lane, d : d + 1] = row + packed[9:10, cols] if d == 0 else row
            for n in range(16):
                reach_ref[r, lane, n] = jnp.exp(-wide(decay[n : n + 1]) * chunk_of)


def copy(source, target, sem):
    pltpu.make_async_copy(source, target, sem).start()


def wait_for(ref, sem):
    pltpu.make_async_copy(ref, ref, sem).wait()


def start_rows(row_refs, x, sem):
    high = row_refs[0].shape[0]
    for i, ref in enumerate(row_refs):
        copy(ref, x.at[pl.ds(i * high, high)], sem)


def start_weights(order, w_ref, stream, block, w, sem):
    if len(w_ref.shape) == 3:
        copy(w_ref.at[stream], w, sem)
    else:
        depth = w_ref.shape[3]
        for part in range(8):
            copy(w_ref.at[order[block], part, stream], w.at[pl.ds(part * depth, depth)], sem)


def dot(a, b):
    return jnp.dot(a, b, preferred_element_type=F32)


def project(x, w, scratch):
    total = dot(x[...], w[...]).astype(BF16).astype(F32)
    lanes, seqs = scratch.shape[:2]
    first_row = lax.broadcasted_iota(jnp.int32, (8, 128), 0) == 0
    for lane in range(lanes):
        cols = slice(lane * 128, (lane + 1) * 128)
        for s in range(seqs):
            first = s * (HEAD + 8 * CHUNK) + HEAD
            edge = total[first - 8 : first, cols]
            for back in (1, 2):
                last = total[first + 8 * (CHUNK - back) : first + 8 * (CHUNK - back) + 8, cols]
                scratch[lane, s, 2 - back] = jnp.where(first_row, pltpu.roll(edge, back, 0), pltpu.roll(last, 1, 0))
            scratch[lane, s, 2:] = total[first : first + 8 * CHUNK, cols].reshape(CHUNK, 8, 128)


def both(first, second):
    return jnp.concatenate([first, second], axis=0).astype(BF16)


def halves(pair):
    pair = pair.astype(F32)
    return pair[:8], pair[8:]


def wide(row):
    return jnp.broadcast_to(row, (8, 128))


def each_unit(scratch, body):
    lanes, seqs = scratch.shape[:2]

    def step(i, carry):
        body(i // seqs, i % seqs)
        return carry

    lax.fori_loop(0, lanes * seqs, step, 0)


def kv_kernel(first, seqs, order, w_ref, *refs):
    row_refs, refs = refs[:seqs], refs[seqs:]
    taps_ref, kern_ref, pole_ref, jump_ref, y_out, e_out, t_ref, x, w, fk, fv, ys, es, row_sem, w_sems, out_sems = refs
    blocks = w.shape[0]
    for block in range(blocks):
        for i, stream in enumerate((KEY, VALUE)):
            start_weights(order, w_ref, stream, block + first, w.at[block, i], w_sems.at[block])
        if block == 0:
            start_rows(row_refs, x, row_sem)
    first_row = lax.broadcasted_iota(jnp.int32, (8, 128), 0)
    wait_for(x, row_sem)

    def each_block(block, carry):
        wait_for(w.at[block], w_sems.at[block])
        project(x, w.at[block, 0], fk)
        project(x, w.at[block, 1], fv)
        c = block + first

        def unit(lane, s):
            tap = lambda j, stream: wide(taps_ref[c, lane, pl.ds(3 * j + stream, 1), :])
            kt = [tap(j, KEY) for j in range(3)]
            vt = [tap(j, VALUE) for j in range(3)]
            kx = [fk[lane, s, t] for t in range(CHUNK + 2)]
            vx = [fv[lane, s, t] for t in range(CHUNK + 2)]
            xs = []
            for t in range(CHUNK):
                k = kt[0] * kx[t + 2] + kt[1] * kx[t + 1] + kt[2] * kx[t]
                v = vt[0] * vx[t + 2] + vt[1] * vx[t + 1] + vt[2] * vx[t]
                xs.append(k * v)
            kern = [wide(kern_ref[c, lane, pl.ds(d, 1), :]) for d in range(CHUNK)]
            for t in range(0, CHUNK, 2):
                pair = []
                for u in (t, t + 1):
                    y = kern[0] * xs[u]
                    for d in range(1, u + 1):
                        y += kern[d] * xs[u - d]
                    pair.append(y)
                ys[block, lane, s, t // 2] = both(*pair)
            for n in range(0, 16, 2):
                pair = []
                for m in (n, n + 1):
                    pole = wide(pole_ref[c, lane, pl.ds(m, 1), :])
                    state = xs[0]
                    for t in range(1, CHUNK):
                        state = pole * state + xs[t]
                    for j, step in enumerate((1, 2, 4)):
                        jump = wide(jump_ref[c, lane, j, pl.ds(m, 1), :])
                        moved = jnp.where(first_row >= step, pltpu.roll(state, step, 0), 0.0)
                        state = state + jump * moved
                    pair.append(jnp.where(first_row >= 1, pltpu.roll(state, 1, 0), 0.0))
                    t_ref[block, lane, s, pl.ds(m, 1), :] = state[7:8, :]
                es[block, lane, s, n // 2] = both(*pair)

        each_unit(fk, unit)
        copy(ys.at[block], y_out.at[block], out_sems.at[0])
        copy(es.at[block], e_out.at[block], out_sems.at[1])
        return carry

    lax.fori_loop(0, blocks, each_block, 0)
    wait_for(ys, out_sems.at[0])
    wait_for(es, out_sems.at[1])


def q_kernel(first, seqs, order, w_ref, *refs):
    row_refs, refs = refs[:seqs], refs[seqs:]
    taps_ref, q_out, x, w, fq, qs, row_sem, w_sems, out_sem = refs
    blocks = w.shape[0]
    for block in range(blocks):
        start_weights(order, w_ref, QUERY, block + first, w.at[block], w_sems.at[block])
        if block == 0:
            start_rows(row_refs, x, row_sem)
    wait_for(x, row_sem)

    def each_block(block, carry):
        wait_for(w.at[block], w_sems.at[block])
        project(x, w.at[block], fq)

        def unit(lane, s):
            qt = [wide(taps_ref[block + first, lane, pl.ds(3 * j + QUERY, 1), :]) for j in range(3)]
            qx = [fq[lane, s, t] for t in range(CHUNK + 2)]
            q = [qt[0] * qx[t + 2] + qt[1] * qx[t + 1] + qt[2] * qx[t] for t in range(CHUNK)]
            for t in range(0, CHUNK, 2):
                qs[block, lane, s, t // 2] = both(q[t], q[t + 1])

        each_unit(fq, unit)
        copy(qs.at[block], q_out.at[block], out_sem)
        return carry

    lax.fori_loop(0, blocks, each_block, 0)
    wait_for(qs, out_sem)


def gate_kernel(y_ref, e_ref, q_ref, in_ref, pole_ref, res_ref, reach_ref, out_ref, gated):
    def unit(s, carry):
        poles, states = [], []
        for n in range(0, 16, 2):
            for m, state in zip((n, n + 1), halves(e_ref[0, 0, s, n // 2])):
                pole = wide(pole_ref[0, 0, pl.ds(m, 1), :])
                state = state + reach_ref[0, 0, m] * wide(in_ref[0, 0, s, pl.ds(m, 1), :])
                poles.append(pole)
                states.append(wide(res_ref[0, 0, pl.ds(m, 1), :]) * pole * state)
        for t in range(0, CHUNK, 2):
            for u, y, q in zip((t, t + 1), halves(y_ref[0, 0, s, t // 2]), halves(q_ref[0, 0, s, t // 2])):
                total = y
                for n in range(16):
                    total += states[n]
                gated[s, pl.ds(u, 8, stride=CHUNK), :] = total * q
                states = [pole * state for pole, state in zip(poles, states)]
        return carry

    lax.fori_loop(0, gated.shape[0], unit, 0)
    out_ref[0] = gated[...].astype(BF16)


def out_kernel(seqs, order, own_ref, others_ref, w_ref, *refs):
    outs, (w, rows, sums, row_sem, w_sems, out_sems) = refs[: 2 * len(seqs)], refs[2 * len(seqs) :]
    length, channels = own_ref.shape[2:]
    tiles = w.shape[0]
    for r in range(4):
        cols = pl.ds(pl.multiple_of(order[r] * channels, channels), channels)
        for i, s in enumerate(seqs):
            source = own_ref.at[0, s] if r == 0 else others_ref.at[r - 1, s]
            copy(source, rows.at[pl.ds(i * length, length), cols], row_sem)
    for t in range(tiles):
        copy(w_ref.at[:, t // 2, pl.ds(t % 2 * channels, channels)], w.at[t], w_sems.at[t])
    wait_for(rows, row_sem)
    for half in range(2):

        def each_tile(i, carry, half=half):
            t = half * (tiles // 2) + i
            wait_for(w.at[t], w_sems.at[t])
            total = dot(rows[...], w[t].reshape(rows.shape[1], channels)).astype(BF16)
            for s in range(len(seqs)):
                there = pl.ds(pl.multiple_of(i * channels, channels), channels)
                sums[half, s, :, there] = total[s * length : (s + 1) * length]
            return carry

        lax.fori_loop(0, tiles // 2, each_tile, 0)
        for s in range(len(seqs)):
            copy(sums.at[half, s], outs[2 * s + half], out_sems.at[half])
    for half in range(2):
        wait_for(sums.at[half], out_sems.at[half])


def carry_states(ends, span):
    core = lax.axis_index("c")
    span = span[:, :, None]
    sent = ends.astype(BF16)
    other = from_ahead(sent, "c", 1).astype(F32)
    sent = sent.astype(F32)
    front, back = jnp.where(core == 0, sent, other), jnp.where(core == 0, other, sent)
    chip = (span * front + back).astype(BF16)
    hops = [from_behind(chip, "y", step).astype(F32) for step in (1, 2, 3)]
    square = span * span
    incoming = hops[0] + square * (hops[1] + square * hops[2])
    return jnp.where(core == 0, incoming, span * incoming + front)


IN_PLACE = pl.BlockSpec(memory_space=pl.ANY)
IN_VMEM = pl.BlockSpec(memory_space=pltpu.VMEM)
IN_SMEM = pl.BlockSpec(memory_space=pltpu.SMEM)
DMA = pltpu.SemaphoreType.DMA


def keys_values(order, w, rows, first, blocks, coefficients, name):
    seqs, (high, width) = len(rows), rows[0].shape
    lanes = coefficients[0].shape[1]
    by_chunk = (blocks, lanes, seqs, CHUNK // 2, 16, 128)
    features = pltpu.VMEM((lanes, seqs, CHUNK + 2, 8, 128), F32)
    return pl.pallas_call(
        functools.partial(kv_kernel, first, seqs),
        in_specs=[IN_SMEM] + [IN_PLACE] * (1 + seqs) + [IN_VMEM] * 4,
        out_specs=[IN_PLACE, IN_PLACE, IN_VMEM],
        scratch_shapes=[
            pltpu.VMEM((seqs * high, width), BF16),
            pltpu.VMEM((blocks, 2, width, lanes * 128), BF16),
            features,
            features,
            pltpu.VMEM(by_chunk, BF16),
            pltpu.VMEM(by_chunk, BF16),
            DMA,
            DMA((blocks,)),
            DMA((2,)),
        ],
        out_shape=[
            jax.ShapeDtypeStruct(by_chunk, BF16),
            jax.ShapeDtypeStruct(by_chunk, BF16),
            jax.ShapeDtypeStruct((blocks, lanes, seqs, 16, 128), F32),
        ],
        compiler_params=compiler_params(),
        name=name,
    )(order, w, *rows, *coefficients)


def queries(order, w, rows, first, blocks, taps, name):
    seqs, (high, width) = len(rows), rows[0].shape
    lanes = taps.shape[1]
    by_chunk = (blocks, lanes, seqs, CHUNK // 2, 16, 128)
    return pl.pallas_call(
        functools.partial(q_kernel, first, seqs),
        in_specs=[IN_SMEM] + [IN_PLACE] * (1 + seqs) + [IN_VMEM],
        out_specs=IN_PLACE,
        scratch_shapes=[
            pltpu.VMEM((seqs * high, width), BF16),
            pltpu.VMEM((blocks, width, lanes * 128), BF16),
            pltpu.VMEM((lanes, seqs, CHUNK + 2, 8, 128), F32),
            pltpu.VMEM(by_chunk, BF16),
            DMA,
            DMA((blocks,)),
            DMA,
        ],
        out_shape=jax.ShapeDtypeStruct(by_chunk, BF16),
        compiler_params=compiler_params(),
        name=name,
    )(order, w, *rows, taps)


def gate(y, e, query, first, coefficients, name):
    blocks, lanes, seqs = y.shape[:3]
    length = CHUNK * 8
    at = lambda a, first: pl.BlockSpec((1, 1) + a.shape[2:], lambda r, lane: (r + first, lane) + (0,) * (a.ndim - 2))
    return pl.pallas_call(
        gate_kernel,
        grid=(blocks, lanes),
        in_specs=[at(a, 0) for a in (y, e, query)] + [at(a, first) for a in coefficients],
        out_specs=pl.BlockSpec((1, seqs, length, 128), lambda r, lane: (r, 0, 0, lane)),
        scratch_shapes=[pltpu.VMEM((seqs, length, 128), F32)],
        out_shape=jax.ShapeDtypeStruct((blocks, seqs, length, lanes * 128), BF16),
        compiler_params=compiler_params(),
        name=name,
    )(y, e, query, *coefficients)


def project_out(order, seqs, own, others, w, name):
    length, channels = own.shape[2:]
    blocks, half = w.shape[0], w.shape[1] * channels
    return pl.pallas_call(
        functools.partial(out_kernel, seqs),
        in_specs=[IN_SMEM] + [IN_PLACE] * 3,
        out_specs=[IN_PLACE] * (2 * len(seqs)),
        scratch_shapes=[
            pltpu.VMEM((2 * w.shape[1], blocks, channels, channels), BF16),
            pltpu.VMEM((len(seqs) * length, blocks * channels), BF16),
            pltpu.VMEM((2, len(seqs), length, half), BF16),
            DMA,
            DMA((2 * w.shape[1],)),
            DMA((2,)),
        ],
        out_shape=[jax.ShapeDtypeStruct((length, half), BF16)] * (2 * len(seqs)),
        compiler_params=compiler_params(),
        name=name,
    )(order, own, others, w)


def shards(tokens, norm_gain, w_in, taps, decay_rate, residues, skip_gain, w_out):
    z, core = lax.axis_index("z"), lax.axis_index("c")
    part = lax.axis_index("y") * 2 + core
    width, _, channels = w_in.shape
    length = tokens.shape[1]
    blocks = seqs = len(OFFSETS)
    lanes = channels // 128
    depth = width // 8

    w_streams = w_in.transpose(1, 0, 2)
    with jax.named_scope("gather_in_weights"):
        share = lax.dynamic_slice(w_streams, (0, part * depth, 0), (3, depth, channels))
        w_all = lax.all_gather(share, ("z", "y", "c"), axis=0).reshape(blocks, 8, 3, depth, channels)

    with jax.named_scope("norm"):
        pairs = [(i, i + 1) for i in range(7)]
        edge = lax.ppermute(tokens[0, length - HEAD :], ("y", "c"), pairs)
        normed = pl.pallas_call(
            norm_kernel,
            out_shape=jax.ShapeDtypeStruct((HEAD + length, width), BF16),
            scratch_shapes=[pltpu.VMEM((width // 128, length, 128), F32)],
            compiler_params=compiler_params(),
            name="norm",
        )(edge, tokens, norm_gain[None])

    with jax.named_scope("gather_tokens"):
        rows = gather_along(normed, "x")

    with jax.named_scope("gather_out_weights"):
        w_out, normed = lax.optimization_barrier((w_out, normed))
        out_share = [
            lax.dynamic_slice(w_out, (0, (part * 2 + i) * channels), (channels, channels)) for i in range(2)
        ]
        w_o = lax.all_gather(jnp.concatenate(out_share, axis=0), ("z", "y", "c"), axis=0)
        w_o = w_o.reshape(blocks, 8, 2 * channels, channels)

    with jax.named_scope("coefficients"):
        packed = pl.pallas_call(
            pack_kernel, out_shape=jax.ShapeDtypeStruct((48, channels), F32), name="pack"
        )(taps, decay_rate, residues, skip_gain[None])
        per_pole = jax.ShapeDtypeStruct((blocks, lanes, 16, 128), F32)
        taps_all, kern, pole, jumps, res, reach, span = pl.pallas_call(
            coefficient_kernel,
            out_shape=[
                per_pole,
                per_pole,
                per_pole,
                jax.ShapeDtypeStruct((blocks, lanes, 3, 16, 128), F32),
                per_pole,
                jax.ShapeDtypeStruct((blocks, lanes, 16, 8, 128), F32),
                per_pole,
            ],
            compiler_params=compiler_params(),
            name="coefficients",
        )(*gather_along(packed, "z"))

    order = jnp.stack([(z + step) % 4 for step in OFFSETS]).astype(jnp.int32)
    coefficients = (taps_all, kern, pole, jumps)

    y0, e0, ends0 = keys_values(order, w_streams, rows, 0, 1, coefficients, "own_keys_values")
    query0 = queries(order, w_streams, rows, 0, 1, taps_all, "own_queries")
    y0, e0, ends0, query0, w_all = lax.optimization_barrier((y0, e0, ends0, query0, w_all))

    y, e, ends = keys_values(order, w_all, rows, 1, 3, coefficients, "keys_values")
    with jax.named_scope("states"):
        incoming = carry_states(jnp.concatenate([ends0, ends], axis=0), span)
    query = queries(order, w_all, rows, 1, 3, taps_all, "queries")
    coefficients = (incoming, pole, res, reach)
    own_gated = gate(y0, e0, query0, 0, coefficients, "own_gate")
    gated = gate(y, e, query, 1, coefficients, "gate")

    far, far_b = project_out(order, (3,), own_gated, gated, w_o, "project_far")
    far, far_b, gated = lax.optimization_barrier((far, far_b, gated))
    own, own_b, near, near_b, back, back_b = project_out(order, (0, 1, 2), own_gated, gated, w_o, "project_out")

    with jax.named_scope("sum_parts"):
        passing, passing_b = from_ahead(far, "x", -1), from_ahead(far_b, "x", 1)
        direct_b, direct = from_ahead(near_b, "x", -1), from_ahead(back, "x", 1)
        added = (near.astype(F32) + passing.astype(F32)).astype(BF16)
        added_b = (back_b.astype(F32) + passing_b.astype(F32)).astype(BF16)
        added, added_b = from_ahead(added, "x", -1), from_ahead(added_b, "x", 1)
        others = jnp.concatenate(
            [added.astype(F32) + direct.astype(F32), added_b.astype(F32) + direct_b.astype(F32)], axis=1
        )
        own = jnp.concatenate([own, own_b], axis=1)
        return (tokens[0].astype(F32) + own.astype(F32) + others).astype(BF16)[None]


def solution(mesh):
    fine = Mesh(mesh.devices.reshape(4, 4, 4, 2), ("x", "z", "y", "c"))
    fsdp, ctx = ("x", "z"), ("y", "c")
    in_specs = (
        P(fsdp, ctx, None),
        P(),
        P(None, None, fsdp),
        P(None, None, fsdp),
        P(None, fsdp),
        P(None, fsdp),
        P(fsdp),
        P(fsdp, None),
    )
    return jax.shard_map(shards, mesh=fine, in_specs=in_specs, out_specs=P(fsdp, ctx, None), check_vma=False)
```

```python
import functools

import jax
import jax.numpy as jnp
from jax import lax
from jax.experimental import pallas as pl
from jax.experimental.pallas import tpu as pltpu
from jax.sharding import Mesh, PartitionSpec as P

F32 = jnp.float32
BF16 = jnp.bfloat16
OFFSETS = (0, 1, 3, 2)
CHUNK = 16
HEAD = 16
QUERY, KEY, VALUE = 0, 1, 2


def from_ahead(value, axis, steps):
    count = lax.axis_size(axis)
    return lax.ppermute(value, axis, [(i, (i - steps) % count) for i in range(count)])


def from_behind(value, axis, steps):
    count = lax.axis_size(axis)
    return lax.ppermute(value, axis, [(i, i + steps) for i in range(count - steps)])


def gather_along(value, axis):
    return [value] + [from_ahead(value, axis, step) for step in OFFSETS[1:]]


def compiler_params():
    return pltpu.CompilerParams(vmem_limit_bytes=60 * 1024 * 1024)


def norm_kernel(edge_ref, tokens_ref, gain_ref, out_ref, natural):
    def normed(rows):
        values = rows.astype(F32)
        inverse_rms = lax.rsqrt(jnp.mean(values * values, axis=-1, keepdims=True) + 1e-06)
        return values * inverse_rms * gain_ref[...]

    out_ref[:HEAD] = normed(edge_ref[...]).astype(BF16)
    values = normed(tokens_ref[0])
    for lane in range(natural.shape[0]):
        cols = slice(lane * 128, (lane + 1) * 128)
        natural[lane] = values[:, cols]
        for t in range(0, CHUNK, 2):
            pair = [natural[lane, pl.ds(t + i, 8, stride=CHUNK), :] for i in range(2)]
            out_ref[HEAD + 8 * t : HEAD + 8 * t + 16, cols] = jnp.concatenate(pair, axis=0).astype(BF16)


def pack_kernel(taps_ref, decay_ref, res_ref, skip_ref, out_ref):
    out_ref[...] = jnp.zeros_like(out_ref)
    for j in range(3):
        out_ref[3 * j : 3 * j + 3] = taps_ref[j]
    out_ref[16:32] = decay_ref[...]
    out_ref[32:48] = res_ref[...]
    out_ref[9:10] = skip_ref[...]


def coefficient_kernel(p0, p1, p2, p3, taps_ref, kern_ref, pole_ref, jump_ref, res_ref, reach_ref, span_ref):
    chunk_of = lax.broadcasted_iota(jnp.int32, (8, 128), 0).astype(F32) * CHUNK
    for r, packed in enumerate((p0, p1, p2, p3)):
        for lane in range(2):
            cols = slice(lane * 128, (lane + 1) * 128)
            decay, res = packed[16:32, cols], packed[32:48, cols]
            taps_ref[r, lane] = packed[0:16, cols]
            pole_ref[r, lane] = jnp.exp(-decay)
            res_ref[r, lane] = res
            span_ref[r, lane] = jnp.exp(-decay * (8 * CHUNK))
            for j in range(3):
                jump_ref[r, lane, j] = jnp.exp(-decay * (CHUNK << j))
            for d in range(CHUNK):
                row = jnp.sum(res * jnp.exp(-decay * d), axis=0, keepdims=True)
                kern_ref[r, lane, d : d + 1] = row + packed[9:10, cols] if d == 0 else row
            for n in range(16):
                reach_ref[r, lane, n] = jnp.exp(-wide(decay[n : n + 1]) * chunk_of)


def copy(source, target, sem):
    pltpu.make_async_copy(source, target, sem).start()


def wait_for(ref, sem):
    pltpu.make_async_copy(ref, ref, sem).wait()


def start_rows(row_refs, x, sem):
    high = row_refs[0].shape[0]
    for i, ref in enumerate(row_refs):
        copy(ref, x.at[pl.ds(i * high, high)], sem)


def start_weights(order, w_ref, stream, block, w, sem):
    if len(w_ref.shape) == 3:
        copy(w_ref.at[stream], w, sem)
    else:
        depth = w_ref.shape[3]
        for part in range(8):
            copy(w_ref.at[order[block], part, stream], w.at[pl.ds(part * depth, depth)], sem)


def dot(a, b):
    return jnp.dot(a, b, preferred_element_type=F32)


def project(x, w, scratch):
    total = dot(x[...], w[...]).astype(BF16).astype(F32)
    lanes, seqs = scratch.shape[:2]
    first_row = lax.broadcasted_iota(jnp.int32, (8, 128), 0) == 0
    for lane in range(lanes):
        cols = slice(lane * 128, (lane + 1) * 128)
        for s in range(seqs):
            first = s * (HEAD + 8 * CHUNK) + HEAD
            edge = total[first - 8 : first, cols]
            for back in (1, 2):
                last = total[first + 8 * (CHUNK - back) : first + 8 * (CHUNK - back) + 8, cols]
                scratch[lane, s, 2 - back] = jnp.where(first_row, pltpu.roll(edge, back, 0), pltpu.roll(last, 1, 0))
            scratch[lane, s, 2:] = total[first : first + 8 * CHUNK, cols].reshape(CHUNK, 8, 128)


def both(first, second):
    return jnp.concatenate([first, second], axis=0).astype(BF16)


def halves(pair):
    pair = pair.astype(F32)
    return pair[:8], pair[8:]


def wide(row):
    return jnp.broadcast_to(row, (8, 128))


def each_unit(scratch, body):
    lanes, seqs = scratch.shape[:2]

    def step(i, carry):
        body(i // seqs, i % seqs)
        return carry

    lax.fori_loop(0, lanes * seqs, step, 0)


def kv_kernel(first, seqs, order, w_ref, *refs):
    row_refs, refs = refs[:seqs], refs[seqs:]
    taps_ref, kern_ref, pole_ref, jump_ref, y_out, e_out, t_ref, x, w, fk, fv, ys, es, row_sem, w_sems, out_sems = refs
    blocks = w.shape[0]
    for block in range(blocks):
        for i, stream in enumerate((KEY, VALUE)):
            start_weights(order, w_ref, stream, block + first, w.at[block, i], w_sems.at[block])
        if block == 0:
            start_rows(row_refs, x, row_sem)
    first_row = lax.broadcasted_iota(jnp.int32, (8, 128), 0)
    wait_for(x, row_sem)

    def each_block(block, carry):
        wait_for(w.at[block], w_sems.at[block])
        project(x, w.at[block, 0], fk)
        project(x, w.at[block, 1], fv)
        c = block + first

        def unit(lane, s):
            tap = lambda j, stream: wide(taps_ref[c, lane, pl.ds(3 * j + stream, 1), :])
            kt = [tap(j, KEY) for j in range(3)]
            vt = [tap(j, VALUE) for j in range(3)]
            kx = [fk[lane, s, t] for t in range(CHUNK + 2)]
            vx = [fv[lane, s, t] for t in range(CHUNK + 2)]
            xs = []
            for t in range(CHUNK):
                k = kt[0] * kx[t + 2] + kt[1] * kx[t + 1] + kt[2] * kx[t]
                v = vt[0] * vx[t + 2] + vt[1] * vx[t + 1] + vt[2] * vx[t]
                xs.append(k * v)
            kern = [wide(kern_ref[c, lane, pl.ds(d, 1), :]) for d in range(CHUNK)]
            for t in range(0, CHUNK, 2):
                pair = []
                for u in (t, t + 1):
                    y = kern[0] * xs[u]
                    for d in range(1, u + 1):
                        y += kern[d] * xs[u - d]
                    pair.append(y)
                ys[block, lane, s, t // 2] = both(*pair)
            for n in range(0, 16, 2):
                pair = []
                for m in (n, n + 1):
                    pole = wide(pole_ref[c, lane, pl.ds(m, 1), :])
                    state = xs[0]
                    for t in range(1, CHUNK):
                        state = pole * state + xs[t]
                    for j, step in enumerate((1, 2, 4)):
                        jump = wide(jump_ref[c, lane, j, pl.ds(m, 1), :])
                        moved = jnp.where(first_row >= step, pltpu.roll(state, step, 0), 0.0)
                        state = state + jump * moved
                    pair.append(jnp.where(first_row >= 1, pltpu.roll(state, 1, 0), 0.0))
                    t_ref[block, lane, s, pl.ds(m, 1), :] = state[7:8, :]
                es[block, lane, s, n // 2] = both(*pair)

        each_unit(fk, unit)
        copy(ys.at[block], y_out.at[block], out_sems.at[0])
        copy(es.at[block], e_out.at[block], out_sems.at[1])
        return carry

    lax.fori_loop(0, blocks, each_block, 0)
    wait_for(ys, out_sems.at[0])
    wait_for(es, out_sems.at[1])


def q_kernel(first, seqs, order, w_ref, *refs):
    row_refs, refs = refs[:seqs], refs[seqs:]
    taps_ref, q_out, x, w, fq, qs, row_sem, w_sems, out_sem = refs
    blocks = w.shape[0]
    for block in range(blocks):
        start_weights(order, w_ref, QUERY, block + first, w.at[block], w_sems.at[block])
        if block == 0:
            start_rows(row_refs, x, row_sem)
    wait_for(x, row_sem)

    def each_block(block, carry):
        wait_for(w.at[block], w_sems.at[block])
        project(x, w.at[block], fq)

        def unit(lane, s):
            qt = [wide(taps_ref[block + first, lane, pl.ds(3 * j + QUERY, 1), :]) for j in range(3)]
            qx = [fq[lane, s, t] for t in range(CHUNK + 2)]
            q = [qt[0] * qx[t + 2] + qt[1] * qx[t + 1] + qt[2] * qx[t] for t in range(CHUNK)]
            for t in range(0, CHUNK, 2):
                qs[block, lane, s, t // 2] = both(q[t], q[t + 1])

        each_unit(fq, unit)
        copy(qs.at[block], q_out.at[block], out_sem)
        return carry

    lax.fori_loop(0, blocks, each_block, 0)
    wait_for(qs, out_sem)


def gate_kernel(y_ref, e_ref, q_ref, in_ref, pole_ref, res_ref, reach_ref, out_ref, gated):
    def unit(s, carry):
        poles, states = [], []
        for n in range(0, 16, 2):
            for m, state in zip((n, n + 1), halves(e_ref[0, 0, s, n // 2])):
                pole = wide(pole_ref[0, 0, pl.ds(m, 1), :])
                state = state + reach_ref[0, 0, m] * wide(in_ref[0, 0, s, pl.ds(m, 1), :])
                poles.append(pole)
                states.append(wide(res_ref[0, 0, pl.ds(m, 1), :]) * pole * state)
        for t in range(0, CHUNK, 2):
            for u, y, q in zip((t, t + 1), halves(y_ref[0, 0, s, t // 2]), halves(q_ref[0, 0, s, t // 2])):
                total = y
                for n in range(16):
                    total += states[n]
                gated[s, pl.ds(u, 8, stride=CHUNK), :] = total * q
                states = [pole * state for pole, state in zip(poles, states)]
        return carry

    lax.fori_loop(0, gated.shape[0], unit, 0)
    out_ref[0] = gated[...].astype(BF16)


def out_kernel(seqs, order, own_ref, others_ref, w_ref, *refs):
    outs, (w, rows, sums, row_sem, w_sems, out_sems) = refs[: 2 * len(seqs)], refs[2 * len(seqs) :]
    length, channels = own_ref.shape[2:]
    tiles, _, _, cols = w.shape
    for r in range(4):
        block = pl.ds(pl.multiple_of(order[r] * channels, channels), channels)
        for i, s in enumerate(seqs):
            source = own_ref.at[0, s] if r == 0 else others_ref.at[r - 1, s]
            copy(source, rows.at[pl.ds(i * length, length), block], row_sem)
    for t in range(tiles):
        copy(w_ref.at[:, :, pl.ds(t * cols, cols)], w.at[t], w_sems.at[t])
    wait_for(rows, row_sem)
    for half in range(2):

        def each_tile(i, carry, half=half):
            t = half * (tiles // 2) + i
            wait_for(w.at[t], w_sems.at[t])
            total = dot(rows[...], w[t].reshape(rows.shape[1], cols)).astype(BF16)
            for s in range(len(seqs)):
                there = pl.ds(pl.multiple_of(i * cols, cols), cols)
                sums[half, s, :, there] = total[s * length : (s + 1) * length]
            return carry

        lax.fori_loop(0, tiles // 2, each_tile, 0)
        for s in range(len(seqs)):
            copy(sums.at[half, s], outs[2 * s + half], out_sems.at[half])
    for half in range(2):
        wait_for(sums.at[half], out_sems.at[half])


def carry_states(ends, span):
    core = lax.axis_index("c")
    span = span[:, :, None]
    sent = ends.astype(BF16)
    other = from_ahead(sent, "c", 1).astype(F32)
    sent = sent.astype(F32)
    front, back = jnp.where(core == 0, sent, other), jnp.where(core == 0, other, sent)
    chip = (span * front + back).astype(BF16)
    hops = [from_behind(chip, "y", step).astype(F32) for step in (1, 2, 3)]
    square = span * span
    incoming = hops[0] + square * (hops[1] + square * hops[2])
    return jnp.where(core == 0, incoming, span * incoming + front)


IN_PLACE = pl.BlockSpec(memory_space=pl.ANY)
IN_VMEM = pl.BlockSpec(memory_space=pltpu.VMEM)
IN_SMEM = pl.BlockSpec(memory_space=pltpu.SMEM)
DMA = pltpu.SemaphoreType.DMA


def keys_values(order, w, rows, first, blocks, coefficients, name):
    seqs, (high, width) = len(rows), rows[0].shape
    lanes = coefficients[0].shape[1]
    by_chunk = (blocks, lanes, seqs, CHUNK // 2, 16, 128)
    features = pltpu.VMEM((lanes, seqs, CHUNK + 2, 8, 128), F32)
    return pl.pallas_call(
        functools.partial(kv_kernel, first, seqs),
        in_specs=[IN_SMEM] + [IN_PLACE] * (1 + seqs) + [IN_VMEM] * 4,
        out_specs=[IN_PLACE, IN_PLACE, IN_VMEM],
        scratch_shapes=[
            pltpu.VMEM((seqs * high, width), BF16),
            pltpu.VMEM((blocks, 2, width, lanes * 128), BF16),
            features,
            features,
            pltpu.VMEM(by_chunk, BF16),
            pltpu.VMEM(by_chunk, BF16),
            DMA,
            DMA((blocks,)),
            DMA((2,)),
        ],
        out_shape=[
            jax.ShapeDtypeStruct(by_chunk, BF16),
            jax.ShapeDtypeStruct(by_chunk, BF16),
            jax.ShapeDtypeStruct((blocks, lanes, seqs, 16, 128), F32),
        ],
        compiler_params=compiler_params(),
        name=name,
    )(order, w, *rows, *coefficients)


def queries(order, w, rows, first, blocks, taps, name):
    seqs, (high, width) = len(rows), rows[0].shape
    lanes = taps.shape[1]
    by_chunk = (blocks, lanes, seqs, CHUNK // 2, 16, 128)
    return pl.pallas_call(
        functools.partial(q_kernel, first, seqs),
        in_specs=[IN_SMEM] + [IN_PLACE] * (1 + seqs) + [IN_VMEM],
        out_specs=IN_PLACE,
        scratch_shapes=[
            pltpu.VMEM((seqs * high, width), BF16),
            pltpu.VMEM((blocks, width, lanes * 128), BF16),
            pltpu.VMEM((lanes, seqs, CHUNK + 2, 8, 128), F32),
            pltpu.VMEM(by_chunk, BF16),
            DMA,
            DMA((blocks,)),
            DMA,
        ],
        out_shape=jax.ShapeDtypeStruct(by_chunk, BF16),
        compiler_params=compiler_params(),
        name=name,
    )(order, w, *rows, taps)


def gate(y, e, query, first, coefficients, name):
    blocks, lanes, seqs = y.shape[:3]
    length = CHUNK * 8
    at = lambda a, first: pl.BlockSpec((1, 1) + a.shape[2:], lambda r, lane: (r + first, lane) + (0,) * (a.ndim - 2))
    return pl.pallas_call(
        gate_kernel,
        grid=(blocks, lanes),
        in_specs=[at(a, 0) for a in (y, e, query)] + [at(a, first) for a in coefficients],
        out_specs=pl.BlockSpec((1, seqs, length, 128), lambda r, lane: (r, 0, 0, lane)),
        scratch_shapes=[pltpu.VMEM((seqs, length, 128), F32)],
        out_shape=jax.ShapeDtypeStruct((blocks, seqs, length, lanes * 128), BF16),
        compiler_params=compiler_params(),
        name=name,
    )(y, e, query, *coefficients)


def project_out(order, seqs, own, others, w, name):
    length, channels = own.shape[2:]
    blocks, half = w.shape[0], w.shape[2] // 2
    cols = 4 * channels
    tiles = w.shape[2] // cols
    return pl.pallas_call(
        functools.partial(out_kernel, seqs),
        in_specs=[IN_SMEM] + [IN_PLACE] * 3,
        out_specs=[IN_PLACE] * (2 * len(seqs)),
        scratch_shapes=[
            pltpu.VMEM((tiles, blocks, channels, cols), BF16),
            pltpu.VMEM((len(seqs) * length, blocks * channels), BF16),
            pltpu.VMEM((2, len(seqs), length, half), BF16),
            DMA,
            DMA((tiles,)),
            DMA((2,)),
        ],
        out_shape=[jax.ShapeDtypeStruct((length, half), BF16)] * (2 * len(seqs)),
        compiler_params=compiler_params(),
        name=name,
    )(order, own, others, w)


def shards(tokens, norm_gain, w_in, taps, decay_rate, residues, skip_gain, w_out):
    z, core = lax.axis_index("z"), lax.axis_index("c")
    part = lax.axis_index("y") * 2 + core
    width, _, channels = w_in.shape
    length = tokens.shape[1]
    blocks = seqs = len(OFFSETS)
    lanes = channels // 128
    depth = width // 8

    w_streams = w_in.transpose(1, 0, 2)
    with jax.named_scope("gather_in_weights"):
        share = lax.dynamic_slice(w_streams, (0, part * depth, 0), (3, depth, channels))
        w_all = lax.all_gather(share, ("z", "y", "c"), axis=0).reshape(blocks, 8, 3, depth, channels)

    with jax.named_scope("norm"):
        pairs = [(i, i + 1) for i in range(7)]
        edge = lax.ppermute(tokens[0, length - HEAD :], ("y", "c"), pairs)
        normed = pl.pallas_call(
            norm_kernel,
            out_shape=jax.ShapeDtypeStruct((HEAD + length, width), BF16),
            scratch_shapes=[pltpu.VMEM((width // 128, length, 128), F32)],
            compiler_params=compiler_params(),
            name="norm",
        )(edge, tokens, norm_gain[None])

    with jax.named_scope("gather_tokens"):
        rows = gather_along(normed, "x")

    with jax.named_scope("gather_out_weights"):
        w_out, normed = lax.optimization_barrier((w_out, normed))
        out_share = lax.dynamic_slice(w_out, (core * (channels // 2), 0), (channels // 2, width))
        w_o = lax.all_gather(out_share, ("z", "c"), axis=0).reshape(blocks, channels, width)

    with jax.named_scope("coefficients"):
        packed = pl.pallas_call(
            pack_kernel, out_shape=jax.ShapeDtypeStruct((48, channels), F32), name="pack"
        )(taps, decay_rate, residues, skip_gain[None])
        per_pole = jax.ShapeDtypeStruct((blocks, lanes, 16, 128), F32)
        taps_all, kern, pole, jumps, res, reach, span = pl.pallas_call(
            coefficient_kernel,
            out_shape=[
                per_pole,
                per_pole,
                per_pole,
                jax.ShapeDtypeStruct((blocks, lanes, 3, 16, 128), F32),
                per_pole,
                jax.ShapeDtypeStruct((blocks, lanes, 16, 8, 128), F32),
                per_pole,
            ],
            compiler_params=compiler_params(),
            name="coefficients",
        )(*gather_along(packed, "z"))

    order = jnp.stack([(z + step) % 4 for step in OFFSETS]).astype(jnp.int32)
    coefficients = (taps_all, kern, pole, jumps)

    y0, e0, ends0 = keys_values(order, w_streams, rows, 0, 1, coefficients, "own_keys_values")
    query0 = queries(order, w_streams, rows, 0, 1, taps_all, "own_queries")
    y0, e0, ends0, query0, w_all = lax.optimization_barrier((y0, e0, ends0, query0, w_all))

    y, e, ends = keys_values(order, w_all, rows, 1, 3, coefficients, "keys_values")
    with jax.named_scope("states"):
        incoming = carry_states(jnp.concatenate([ends0, ends], axis=0), span)
    query = queries(order, w_all, rows, 1, 3, taps_all, "queries")
    coefficients = (incoming, pole, res, reach)
    own_gated = gate(y0, e0, query0, 0, coefficients, "own_gate")
    gated = gate(y, e, query, 1, coefficients, "gate")

    far, far_b = project_out(order, (3,), own_gated, gated, w_o, "project_far")
    far, far_b, gated = lax.optimization_barrier((far, far_b, gated))
    own, own_b, near, near_b, back, back_b = project_out(order, (0, 1, 2), own_gated, gated, w_o, "project_out")

    with jax.named_scope("sum_parts"):
        passing, passing_b = from_ahead(far, "x", -1), from_ahead(far_b, "x", 1)
        direct_b, direct = from_ahead(near_b, "x", -1), from_ahead(back, "x", 1)
        added = (near.astype(F32) + passing.astype(F32)).astype(BF16)
        added_b = (back_b.astype(F32) + passing_b.astype(F32)).astype(BF16)
        added, added_b = from_ahead(added, "x", -1), from_ahead(added_b, "x", 1)
        others = jnp.concatenate(
            [added.astype(F32) + direct.astype(F32), added_b.astype(F32) + direct_b.astype(F32)], axis=1
        )
        own = jnp.concatenate([own, own_b], axis=1)
        return (tokens[0].astype(F32) + own.astype(F32) + others).astype(BF16)[None]


def solution(mesh):
    fine = Mesh(mesh.devices.reshape(4, 4, 4, 2), ("x", "z", "y", "c"))
    fsdp, ctx = ("x", "z"), ("y", "c")
    in_specs = (
        P(fsdp, ctx, None),
        P(),
        P(None, None, fsdp),
        P(None, None, fsdp),
        P(None, fsdp),
        P(None, fsdp),
        P(fsdp),
        P(fsdp, None),
    )
    return jax.shard_map(shards, mesh=fine, in_specs=in_specs, out_specs=P(fsdp, ctx, None), check_vma=False)
```

```python
import functools

import jax
import jax.numpy as jnp
from jax import lax
from jax.experimental import pallas as pl
from jax.experimental.pallas import tpu as pltpu
from jax.sharding import Mesh, PartitionSpec as P

F32 = jnp.float32
BF16 = jnp.bfloat16
OFFSETS = (0, 1, 3, 2)
CHUNK = 16
HEAD = 16
QUERY, KEY, VALUE = 0, 1, 2


def from_ahead(value, axis, steps):
    count = lax.axis_size(axis)
    return lax.ppermute(value, axis, [(i, (i - steps) % count) for i in range(count)])


def from_behind(value, axis, steps):
    count = lax.axis_size(axis)
    return lax.ppermute(value, axis, [(i, i + steps) for i in range(count - steps)])


def gather_along(value, axis):
    return [value] + [from_ahead(value, axis, step) for step in OFFSETS[1:]]


def compiler_params():
    return pltpu.CompilerParams(vmem_limit_bytes=60 * 1024 * 1024)


def norm_kernel(edge_ref, tokens_ref, gain_ref, out_ref, natural):
    def normed(rows):
        values = rows.astype(F32)
        inverse_rms = lax.rsqrt(jnp.mean(values * values, axis=-1, keepdims=True) + 1e-06)
        return values * inverse_rms * gain_ref[...]

    out_ref[:HEAD] = normed(edge_ref[...]).astype(BF16)
    values = normed(tokens_ref[0])
    for lane in range(natural.shape[0]):
        cols = slice(lane * 128, (lane + 1) * 128)
        natural[lane] = values[:, cols]
        for t in range(0, CHUNK, 2):
            pair = [natural[lane, pl.ds(t + i, 8, stride=CHUNK), :] for i in range(2)]
            out_ref[HEAD + 8 * t : HEAD + 8 * t + 16, cols] = jnp.concatenate(pair, axis=0).astype(BF16)


def pack_kernel(taps_ref, decay_ref, res_ref, skip_ref, out_ref):
    out_ref[...] = jnp.zeros_like(out_ref)
    for j in range(3):
        out_ref[3 * j : 3 * j + 3] = taps_ref[j]
    out_ref[16:32] = decay_ref[...]
    out_ref[32:48] = res_ref[...]
    out_ref[9:10] = skip_ref[...]


def coefficient_kernel(p0, p1, p2, p3, taps_ref, kern_ref, pole_ref, jump_ref, res_ref, reach_ref, span_ref):
    chunk_of = lax.broadcasted_iota(jnp.int32, (8, 128), 0).astype(F32) * CHUNK
    for r, packed in enumerate((p0, p1, p2, p3)):
        for lane in range(2):
            cols = slice(lane * 128, (lane + 1) * 128)
            decay, res = packed[16:32, cols], packed[32:48, cols]
            taps_ref[r, lane] = packed[0:16, cols]
            pole_ref[r, lane] = jnp.exp(-decay)
            res_ref[r, lane] = res
            span_ref[r, lane] = jnp.exp(-decay * (8 * CHUNK))
            for j in range(3):
                jump_ref[r, lane, j] = jnp.exp(-decay * (CHUNK << j))
            for d in range(CHUNK):
                row = jnp.sum(res * jnp.exp(-decay * d), axis=0, keepdims=True)
                kern_ref[r, lane, d : d + 1] = row + packed[9:10, cols] if d == 0 else row
            for n in range(16):
                reach_ref[r, lane, n] = jnp.exp(-wide(decay[n : n + 1]) * chunk_of)


def copy(source, target, sem):
    pltpu.make_async_copy(source, target, sem).start()


def wait_for(ref, sem):
    pltpu.make_async_copy(ref, ref, sem).wait()


def start_rows(row_refs, x, sem):
    high = row_refs[0].shape[0]
    for i, ref in enumerate(row_refs):
        copy(ref, x.at[pl.ds(i * high, high)], sem)


def start_weights(order, w_ref, stream, block, w, sem):
    if len(w_ref.shape) == 3:
        copy(w_ref.at[stream], w, sem)
    else:
        depth = w_ref.shape[3]
        for part in range(8):
            copy(w_ref.at[order[block], part, stream], w.at[pl.ds(part * depth, depth)], sem)


def dot(a, b):
    return jnp.dot(a, b, preferred_element_type=F32)


def project(x, w, *scratches):
    total = dot(x[...], w[...]).astype(BF16).astype(F32)
    lanes, seqs = scratches[0].shape[:2]
    first_row = lax.broadcasted_iota(jnp.int32, (8, 128), 0) == 0
    for column in range(lanes * len(scratches)):
        scratch, lane = scratches[column // lanes], column % lanes
        cols = slice(column * 128, (column + 1) * 128)
        for s in range(seqs):
            first = s * (HEAD + 8 * CHUNK) + HEAD
            edge = total[first - 8 : first, cols]
            for back in (1, 2):
                last = total[first + 8 * (CHUNK - back) : first + 8 * (CHUNK - back) + 8, cols]
                scratch[lane, s, 2 - back] = jnp.where(first_row, pltpu.roll(edge, back, 0), pltpu.roll(last, 1, 0))
            scratch[lane, s, 2:] = total[first : first + 8 * CHUNK, cols].reshape(CHUNK, 8, 128)


def both(first, second):
    return jnp.concatenate([first, second], axis=0).astype(BF16)


def halves(pair):
    pair = pair.astype(F32)
    return pair[:8], pair[8:]


def wide(row):
    return jnp.broadcast_to(row, (8, 128))


def each_unit(scratch, body):
    lanes, seqs = scratch.shape[:2]

    def step(i, carry):
        body(i // seqs, i % seqs)
        return carry

    lax.fori_loop(0, lanes * seqs, step, 0)


def kv_kernel(first, seqs, order, w_ref, *refs):
    row_refs, refs = refs[:seqs], refs[seqs:]
    taps_ref, kern_ref, pole_ref, jump_ref, y_out, e_out, t_ref, x, w, fk, fv, ys, es, row_sem, w_sems, out_sems = refs
    blocks = w.shape[0]
    for block in range(blocks):
        for i, stream in enumerate((KEY, VALUE)):
            start_weights(order, w_ref, stream, block + first, w.at[block, :, pl.ds(i * 256, 256)], w_sems.at[block])
        if block == 0:
            start_rows(row_refs, x, row_sem)
    first_row = lax.broadcasted_iota(jnp.int32, (8, 128), 0)
    wait_for(x, row_sem)

    def each_block(block, carry):
        wait_for(w.at[block], w_sems.at[block])
        project(x, w.at[block], fk, fv)
        c = block + first

        def unit(lane, s):
            tap = lambda j, stream: wide(taps_ref[c, lane, pl.ds(3 * j + stream, 1), :])
            kt = [tap(j, KEY) for j in range(3)]
            vt = [tap(j, VALUE) for j in range(3)]
            kx = [fk[lane, s, t] for t in range(CHUNK + 2)]
            vx = [fv[lane, s, t] for t in range(CHUNK + 2)]
            xs = []
            for t in range(CHUNK):
                k = kt[0] * kx[t + 2] + kt[1] * kx[t + 1] + kt[2] * kx[t]
                v = vt[0] * vx[t + 2] + vt[1] * vx[t + 1] + vt[2] * vx[t]
                xs.append(k * v)
            kern = [wide(kern_ref[c, lane, pl.ds(d, 1), :]) for d in range(CHUNK)]
            for t in range(0, CHUNK, 2):
                pair = []
                for u in (t, t + 1):
                    y = kern[0] * xs[u]
                    for d in range(1, u + 1):
                        y += kern[d] * xs[u - d]
                    pair.append(y)
                ys[block, lane, s, t // 2] = both(*pair)
            for n in range(0, 16, 2):
                pair = []
                for m in (n, n + 1):
                    pole = wide(pole_ref[c, lane, pl.ds(m, 1), :])
                    state = xs[0]
                    for t in range(1, CHUNK):
                        state = pole * state + xs[t]
                    for j, step in enumerate((1, 2, 4)):
                        jump = wide(jump_ref[c, lane, j, pl.ds(m, 1), :])
                        moved = jnp.where(first_row >= step, pltpu.roll(state, step, 0), 0.0)
                        state = state + jump * moved
                    pair.append(jnp.where(first_row >= 1, pltpu.roll(state, 1, 0), 0.0))
                    t_ref[block, lane, s, pl.ds(m, 1), :] = state[7:8, :]
                es[block, lane, s, n // 2] = both(*pair)

        each_unit(fk, unit)
        copy(ys.at[block], y_out.at[block], out_sems.at[0])
        copy(es.at[block], e_out.at[block], out_sems.at[1])
        return carry

    lax.fori_loop(0, blocks, each_block, 0)
    wait_for(ys, out_sems.at[0])
    wait_for(es, out_sems.at[1])


def q_kernel(first, seqs, order, w_ref, *refs):
    row_refs, refs = refs[:seqs], refs[seqs:]
    taps_ref, q_out, x, w, fq, qs, row_sem, w_sems, out_sem = refs
    blocks = w.shape[0]
    for block in range(blocks):
        start_weights(order, w_ref, QUERY, block + first, w.at[block], w_sems.at[block])
        if block == 0:
            start_rows(row_refs, x, row_sem)
    wait_for(x, row_sem)

    def each_block(block, carry):
        wait_for(w.at[block], w_sems.at[block])
        project(x, w.at[block], fq)

        def unit(lane, s):
            qt = [wide(taps_ref[block + first, lane, pl.ds(3 * j + QUERY, 1), :]) for j in range(3)]
            qx = [fq[lane, s, t] for t in range(CHUNK + 2)]
            q = [qt[0] * qx[t + 2] + qt[1] * qx[t + 1] + qt[2] * qx[t] for t in range(CHUNK)]
            for t in range(0, CHUNK, 2):
                qs[block, lane, s, t // 2] = both(q[t], q[t + 1])

        each_unit(fq, unit)
        copy(qs.at[block], q_out.at[block], out_sem)
        return carry

    lax.fori_loop(0, blocks, each_block, 0)
    wait_for(qs, out_sem)


def gate_kernel(y_ref, e_ref, q_ref, in_ref, pole_ref, res_ref, reach_ref, out_ref, gated):
    def unit(s, carry):
        poles, states = [], []
        for n in range(0, 16, 2):
            for m, state in zip((n, n + 1), halves(e_ref[0, 0, s, n // 2])):
                pole = wide(pole_ref[0, 0, pl.ds(m, 1), :])
                state = state + reach_ref[0, 0, m] * wide(in_ref[0, 0, s, pl.ds(m, 1), :])
                poles.append(pole)
                states.append(wide(res_ref[0, 0, pl.ds(m, 1), :]) * pole * state)
        for t in range(0, CHUNK, 2):
            for u, y, q in zip((t, t + 1), halves(y_ref[0, 0, s, t // 2]), halves(q_ref[0, 0, s, t // 2])):
                total = y
                for n in range(16):
                    total += states[n]
                gated[s, pl.ds(u, 8, stride=CHUNK), :] = total * q
                states = [pole * state for pole, state in zip(poles, states)]
        return carry

    lax.fori_loop(0, gated.shape[0], unit, 0)
    out_ref[0] = gated[...].astype(BF16)


def out_kernel(seqs, order, own_ref, others_ref, w_ref, *refs):
    outs, (w, rows, sums, row_sem, w_sems, out_sems) = refs[: 2 * len(seqs)], refs[2 * len(seqs) :]
    length, channels = own_ref.shape[2:]
    tiles, _, _, cols = w.shape
    for r in range(4):
        block = pl.ds(pl.multiple_of(order[r] * channels, channels), channels)
        for i, s in enumerate(seqs):
            source = own_ref.at[0, s] if r == 0 else others_ref.at[r - 1, s]
            copy(source, rows.at[pl.ds(i * length, length), block], row_sem)
    for t in range(tiles):
        copy(w_ref.at[:, :, pl.ds(t * cols, cols)], w.at[t], w_sems.at[t])
    wait_for(rows, row_sem)
    for half in range(2):

        def each_tile(i, carry, half=half):
            t = half * (tiles // 2) + i
            wait_for(w.at[t], w_sems.at[t])
            total = dot(rows[...], w[t].reshape(rows.shape[1], cols)).astype(BF16)
            for s in range(len(seqs)):
                there = pl.ds(pl.multiple_of(i * cols, cols), cols)
                sums[half, s, :, there] = total[s * length : (s + 1) * length]
            return carry

        lax.fori_loop(0, tiles // 2, each_tile, 0)
        for s in range(len(seqs)):
            copy(sums.at[half, s], outs[2 * s + half], out_sems.at[half])
    for half in range(2):
        wait_for(sums.at[half], out_sems.at[half])


def carry_states(ends, span):
    core = lax.axis_index("c")
    span = span[:, :, None]
    sent = ends.astype(BF16)
    other = from_ahead(sent, "c", 1).astype(F32)
    sent = sent.astype(F32)
    front, back = jnp.where(core == 0, sent, other), jnp.where(core == 0, other, sent)
    chip = (span * front + back).astype(BF16)
    hops = [from_behind(chip, "y", step).astype(F32) for step in (1, 2, 3)]
    square = span * span
    incoming = hops[0] + square * (hops[1] + square * hops[2])
    return jnp.where(core == 0, incoming, span * incoming + front)


IN_PLACE = pl.BlockSpec(memory_space=pl.ANY)
IN_VMEM = pl.BlockSpec(memory_space=pltpu.VMEM)
IN_SMEM = pl.BlockSpec(memory_space=pltpu.SMEM)
DMA = pltpu.SemaphoreType.DMA


def keys_values(order, w, rows, first, blocks, coefficients, name):
    seqs, (high, width) = len(rows), rows[0].shape
    lanes = coefficients[0].shape[1]
    by_chunk = (blocks, lanes, seqs, CHUNK // 2, 16, 128)
    features = pltpu.VMEM((lanes, seqs, CHUNK + 2, 8, 128), F32)
    return pl.pallas_call(
        functools.partial(kv_kernel, first, seqs),
        in_specs=[IN_SMEM] + [IN_PLACE] * (1 + seqs) + [IN_VMEM] * 4,
        out_specs=[IN_PLACE, IN_PLACE, IN_VMEM],
        scratch_shapes=[
            pltpu.VMEM((seqs * high, width), BF16),
            pltpu.VMEM((blocks, width, 2 * lanes * 128), BF16),
            features,
            features,
            pltpu.VMEM(by_chunk, BF16),
            pltpu.VMEM(by_chunk, BF16),
            DMA,
            DMA((blocks,)),
            DMA((2,)),
        ],
        out_shape=[
            jax.ShapeDtypeStruct(by_chunk, BF16),
            jax.ShapeDtypeStruct(by_chunk, BF16),
            jax.ShapeDtypeStruct((blocks, lanes, seqs, 16, 128), F32),
        ],
        compiler_params=compiler_params(),
        name=name,
    )(order, w, *rows, *coefficients)


def queries(order, w, rows, first, blocks, taps, name):
    seqs, (high, width) = len(rows), rows[0].shape
    lanes = taps.shape[1]
    by_chunk = (blocks, lanes, seqs, CHUNK // 2, 16, 128)
    return pl.pallas_call(
        functools.partial(q_kernel, first, seqs),
        in_specs=[IN_SMEM] + [IN_PLACE] * (1 + seqs) + [IN_VMEM],
        out_specs=IN_PLACE,
        scratch_shapes=[
            pltpu.VMEM((seqs * high, width), BF16),
            pltpu.VMEM((blocks, width, lanes * 128), BF16),
            pltpu.VMEM((lanes, seqs, CHUNK + 2, 8, 128), F32),
            pltpu.VMEM(by_chunk, BF16),
            DMA,
            DMA((blocks,)),
            DMA,
        ],
        out_shape=jax.ShapeDtypeStruct(by_chunk, BF16),
        compiler_params=compiler_params(),
        name=name,
    )(order, w, *rows, taps)


def gate(y, e, query, first, coefficients, name):
    blocks, lanes, seqs = y.shape[:3]
    length = CHUNK * 8
    at = lambda a, first: pl.BlockSpec((1, 1) + a.shape[2:], lambda r, lane: (r + first, lane) + (0,) * (a.ndim - 2))
    return pl.pallas_call(
        gate_kernel,
        grid=(blocks, lanes),
        in_specs=[at(a, 0) for a in (y, e, query)] + [at(a, first) for a in coefficients],
        out_specs=pl.BlockSpec((1, seqs, length, 128), lambda r, lane: (r, 0, 0, lane)),
        scratch_shapes=[pltpu.VMEM((seqs, length, 128), F32)],
        out_shape=jax.ShapeDtypeStruct((blocks, seqs, length, lanes * 128), BF16),
        compiler_params=compiler_params(),
        name=name,
    )(y, e, query, *coefficients)


def project_out(order, seqs, own, others, w, name):
    length, channels = own.shape[2:]
    blocks, half = w.shape[0], w.shape[2] // 2
    cols = 8 * channels
    tiles = w.shape[2] // cols
    return pl.pallas_call(
        functools.partial(out_kernel, seqs),
        in_specs=[IN_SMEM] + [IN_PLACE] * 3,
        out_specs=[IN_PLACE] * (2 * len(seqs)),
        scratch_shapes=[
            pltpu.VMEM((tiles, blocks, channels, cols), BF16),
            pltpu.VMEM((len(seqs) * length, blocks * channels), BF16),
            pltpu.VMEM((2, len(seqs), length, half), BF16),
            DMA,
            DMA((tiles,)),
            DMA((2,)),
        ],
        out_shape=[jax.ShapeDtypeStruct((length, half), BF16)] * (2 * len(seqs)),
        compiler_params=compiler_params(),
        name=name,
    )(order, own, others, w)


def shards(tokens, norm_gain, w_in, taps, decay_rate, residues, skip_gain, w_out):
    z, core = lax.axis_index("z"), lax.axis_index("c")
    part = lax.axis_index("y") * 2 + core
    width, _, channels = w_in.shape
    length = tokens.shape[1]
    blocks = seqs = len(OFFSETS)
    lanes = channels // 128
    depth = width // 8

    w_streams = w_in.transpose(1, 0, 2)
    with jax.named_scope("gather_in_weights"):
        share = lax.dynamic_slice(w_streams, (0, part * depth, 0), (3, depth, channels))
        w_all = lax.all_gather(share, ("z", "y", "c"), axis=0).reshape(blocks, 8, 3, depth, channels)

    with jax.named_scope("norm"):
        pairs = [(i, i + 1) for i in range(7)]
        edge = lax.ppermute(tokens[0, length - HEAD :], ("y", "c"), pairs)
        normed = pl.pallas_call(
            norm_kernel,
            out_shape=jax.ShapeDtypeStruct((HEAD + length, width), BF16),
            scratch_shapes=[pltpu.VMEM((width // 128, length, 128), F32)],
            compiler_params=compiler_params(),
            name="norm",
        )(edge, tokens, norm_gain[None])

    with jax.named_scope("gather_tokens"):
        rows = gather_along(normed, "x")

    with jax.named_scope("gather_out_weights"):
        w_out, normed = lax.optimization_barrier((w_out, normed))
        out_share = lax.dynamic_slice(w_out, (core * (channels // 2), 0), (channels // 2, width))
        w_o = lax.all_gather(out_share, ("z", "c"), axis=0).reshape(blocks, channels, width)

    with jax.named_scope("coefficients"):
        packed = pl.pallas_call(
            pack_kernel, out_shape=jax.ShapeDtypeStruct((48, channels), F32), name="pack"
        )(taps, decay_rate, residues, skip_gain[None])
        per_pole = jax.ShapeDtypeStruct((blocks, lanes, 16, 128), F32)
        taps_all, kern, pole, jumps, res, reach, span = pl.pallas_call(
            coefficient_kernel,
            out_shape=[
                per_pole,
                per_pole,
                per_pole,
                jax.ShapeDtypeStruct((blocks, lanes, 3, 16, 128), F32),
                per_pole,
                jax.ShapeDtypeStruct((blocks, lanes, 16, 8, 128), F32),
                per_pole,
            ],
            compiler_params=compiler_params(),
            name="coefficients",
        )(*gather_along(packed, "z"))

    order = jnp.stack([(z + step) % 4 for step in OFFSETS]).astype(jnp.int32)
    coefficients = (taps_all, kern, pole, jumps)

    y0, e0, ends0 = keys_values(order, w_streams, rows, 0, 1, coefficients, "own_keys_values")
    query0 = queries(order, w_streams, rows, 0, 1, taps_all, "own_queries")
    y0, e0, ends0, query0, w_all = lax.optimization_barrier((y0, e0, ends0, query0, w_all))

    y, e, ends = keys_values(order, w_all, rows, 1, 3, coefficients, "keys_values")
    with jax.named_scope("states"):
        incoming = carry_states(jnp.concatenate([ends0, ends], axis=0), span)
    query = queries(order, w_all, rows, 1, 3, taps_all, "queries")
    coefficients = (incoming, pole, res, reach)
    own_gated = gate(y0, e0, query0, 0, coefficients, "own_gate")
    gated = gate(y, e, query, 1, coefficients, "gate")

    far, far_b = project_out(order, (3,), own_gated, gated, w_o, "project_far")
    far, far_b, gated = lax.optimization_barrier((far, far_b, gated))
    own, own_b, near, near_b, back, back_b = project_out(order, (0, 1, 2), own_gated, gated, w_o, "project_out")

    with jax.named_scope("sum_parts"):
        passing, passing_b = from_ahead(far, "x", -1), from_ahead(far_b, "x", 1)
        direct_b, direct = from_ahead(near_b, "x", -1), from_ahead(back, "x", 1)
        added = (near.astype(F32) + passing.astype(F32)).astype(BF16)
        added_b = (back_b.astype(F32) + passing_b.astype(F32)).astype(BF16)
        added, added_b = from_ahead(added, "x", -1), from_ahead(added_b, "x", 1)
        base = tokens[0].astype(F32) + jnp.concatenate([own, own_b], axis=1).astype(F32)
        base = lax.optimization_barrier(base + jnp.concatenate([direct, direct_b], axis=1).astype(F32))
        return (base + jnp.concatenate([added, added_b], axis=1).astype(F32)).astype(BF16)[None]


def solution(mesh):
    fine = Mesh(mesh.devices.reshape(4, 4, 4, 2), ("x", "z", "y", "c"))
    fsdp, ctx = ("x", "z"), ("y", "c")
    in_specs = (
        P(fsdp, ctx, None),
        P(),
        P(None, None, fsdp),
        P(None, None, fsdp),
        P(None, fsdp),
        P(None, fsdp),
        P(fsdp),
        P(fsdp, None),
    )
    return jax.shard_map(shards, mesh=fine, in_specs=in_specs, out_specs=P(fsdp, ctx, None), check_vma=False)
```

```python
import functools

import jax
import jax.numpy as jnp
from jax import lax
from jax.experimental import pallas as pl
from jax.experimental.pallas import tpu as pltpu
from jax.sharding import Mesh, PartitionSpec as P

F32 = jnp.float32
BF16 = jnp.bfloat16
OFFSETS = (0, 1, 3, 2)
CHUNK = 16
HEAD = 16
QUERY, KEY, VALUE = 0, 1, 2


def from_ahead(value, axis, steps):
    count = lax.axis_size(axis)
    return lax.ppermute(value, axis, [(i, (i - steps) % count) for i in range(count)])


def from_behind(value, axis, steps):
    count = lax.axis_size(axis)
    return lax.ppermute(value, axis, [(i, i + steps) for i in range(count - steps)])


def gather_along(value, axis):
    return [value] + [from_ahead(value, axis, step) for step in OFFSETS[1:]]


def compiler_params():
    return pltpu.CompilerParams(vmem_limit_bytes=60 * 1024 * 1024)


def norm_kernel(edge_ref, tokens_ref, gain_ref, out_ref, natural):
    def normed(rows):
        values = rows.astype(F32)
        inverse_rms = lax.rsqrt(jnp.mean(values * values, axis=-1, keepdims=True) + 1e-06)
        return values * inverse_rms * gain_ref[...]

    out_ref[:HEAD] = normed(edge_ref[...]).astype(BF16)
    values = normed(tokens_ref[0])
    for lane in range(natural.shape[0]):
        cols = slice(lane * 128, (lane + 1) * 128)
        natural[lane] = values[:, cols]
        for t in range(0, CHUNK, 2):
            pair = [natural[lane, pl.ds(t + i, 8, stride=CHUNK), :] for i in range(2)]
            out_ref[HEAD + 8 * t : HEAD + 8 * t + 16, cols] = jnp.concatenate(pair, axis=0).astype(BF16)


def pack_kernel(taps_ref, decay_ref, res_ref, skip_ref, out_ref):
    out_ref[...] = jnp.zeros_like(out_ref)
    for j in range(3):
        out_ref[3 * j : 3 * j + 3] = taps_ref[j]
    out_ref[16:32] = decay_ref[...]
    out_ref[32:48] = res_ref[...]
    out_ref[9:10] = skip_ref[...]


def coefficient_kernel(p0, p1, p2, p3, taps_ref, kern_ref, pole_ref, jump_ref, res_ref, reach_ref, span_ref):
    chunk_of = lax.broadcasted_iota(jnp.int32, (8, 128), 0).astype(F32) * CHUNK
    for r, packed in enumerate((p0, p1, p2, p3)):
        for lane in range(2):
            cols = slice(lane * 128, (lane + 1) * 128)
            decay, res = packed[16:32, cols], packed[32:48, cols]
            taps_ref[r, lane] = packed[0:16, cols]
            pole_ref[r, lane] = jnp.exp(-decay)
            res_ref[r, lane] = res
            span_ref[r, lane] = jnp.exp(-decay * (8 * CHUNK))
            for j in range(3):
                jump_ref[r, lane, j] = jnp.exp(-decay * (CHUNK << j))
            for d in range(CHUNK):
                row = jnp.sum(res * jnp.exp(-decay * d), axis=0, keepdims=True)
                kern_ref[r, lane, d : d + 1] = row + packed[9:10, cols] if d == 0 else row
            for n in range(16):
                reach_ref[r, lane, n] = jnp.exp(-wide(decay[n : n + 1]) * chunk_of)


def copy(source, target, sem):
    pltpu.make_async_copy(source, target, sem).start()


def wait_for(ref, sem):
    pltpu.make_async_copy(ref, ref, sem).wait()


def start_rows(row_refs, x, sem):
    high = row_refs[0].shape[0]
    for i, ref in enumerate(row_refs):
        copy(ref, x.at[pl.ds(i * high, high)], sem)


def start_weights(order, w_ref, stream, block, w, sem):
    if len(w_ref.shape) == 3:
        copy(w_ref.at[stream], w, sem)
    else:
        depth = w_ref.shape[3]
        for part in range(8):
            copy(w_ref.at[order[block], part, stream], w.at[pl.ds(part * depth, depth)], sem)


def dot(a, b):
    return jnp.dot(a, b, preferred_element_type=F32)


def project(x, w, *scratches):
    total = dot(x[...], w[...]).astype(BF16).astype(F32)
    lanes, seqs = scratches[0].shape[:2]
    first_row = lax.broadcasted_iota(jnp.int32, (8, 128), 0) == 0
    for column in range(lanes * len(scratches)):
        scratch, lane = scratches[column // lanes], column % lanes
        cols = slice(column * 128, (column + 1) * 128)
        for s in range(seqs):
            first = s * (HEAD + 8 * CHUNK) + HEAD
            edge = total[first - 8 : first, cols]
            for back in (1, 2):
                last = total[first + 8 * (CHUNK - back) : first + 8 * (CHUNK - back) + 8, cols]
                scratch[lane, s, 2 - back] = jnp.where(first_row, pltpu.roll(edge, back, 0), pltpu.roll(last, 1, 0))
            scratch[lane, s, 2:] = total[first : first + 8 * CHUNK, cols].reshape(CHUNK, 8, 128)


def both(first, second):
    return jnp.concatenate([first, second], axis=0).astype(BF16)


def halves(pair):
    pair = pair.astype(F32)
    return pair[:8], pair[8:]


def wide(row):
    return jnp.broadcast_to(row, (8, 128))


def each_unit(scratch, body):
    lanes, seqs = scratch.shape[:2]

    def step(i, carry):
        body(i // seqs, i % seqs)
        return carry

    lax.fori_loop(0, lanes * seqs, step, 0)


def kv_kernel(first, seqs, order, w_ref, *refs):
    row_refs, refs = refs[:seqs], refs[seqs:]
    taps_ref, kern_ref, pole_ref, jump_ref, y_out, e_out, t_ref, x, w, fk, fv, ys, es, row_sem, w_sems, out_sems = refs
    blocks = w.shape[0]
    for block in range(blocks):
        for i, stream in enumerate((KEY, VALUE)):
            start_weights(order, w_ref, stream, block + first, w.at[block, :, pl.ds(i * 256, 256)], w_sems.at[block])
        if block == 0:
            start_rows(row_refs, x, row_sem)
    first_row = lax.broadcasted_iota(jnp.int32, (8, 128), 0)
    wait_for(x, row_sem)

    def each_block(block, carry):
        wait_for(w.at[block], w_sems.at[block])
        project(x, w.at[block], fk, fv)
        c = block + first

        def unit(lane, s):
            tap = lambda j, stream: wide(taps_ref[c, lane, pl.ds(3 * j + stream, 1), :])
            kt = [tap(j, KEY) for j in range(3)]
            vt = [tap(j, VALUE) for j in range(3)]
            kx = [fk[lane, s, t] for t in range(CHUNK + 2)]
            vx = [fv[lane, s, t] for t in range(CHUNK + 2)]
            xs = []
            for t in range(CHUNK):
                k = kt[0] * kx[t + 2] + kt[1] * kx[t + 1] + kt[2] * kx[t]
                v = vt[0] * vx[t + 2] + vt[1] * vx[t + 1] + vt[2] * vx[t]
                xs.append(k * v)
            kern = [wide(kern_ref[c, lane, pl.ds(d, 1), :]) for d in range(CHUNK)]
            for t in range(0, CHUNK, 2):
                pair = []
                for u in (t, t + 1):
                    y = kern[0] * xs[u]
                    for d in range(1, u + 1):
                        y += kern[d] * xs[u - d]
                    pair.append(y)
                ys[block, lane, s, t // 2] = both(*pair)
            for n in range(0, 16, 2):
                pair = []
                for m in (n, n + 1):
                    pole = wide(pole_ref[c, lane, pl.ds(m, 1), :])
                    state = xs[0]
                    for t in range(1, CHUNK):
                        state = pole * state + xs[t]
                    for j, step in enumerate((1, 2, 4)):
                        jump = wide(jump_ref[c, lane, j, pl.ds(m, 1), :])
                        moved = jnp.where(first_row >= step, pltpu.roll(state, step, 0), 0.0)
                        state = state + jump * moved
                    pair.append(jnp.where(first_row >= 1, pltpu.roll(state, 1, 0), 0.0))
                    t_ref[block, lane, s, pl.ds(m, 1), :] = state[7:8, :]
                es[block, lane, s, n // 2] = both(*pair)

        each_unit(fk, unit)
        copy(ys.at[block], y_out.at[block], out_sems.at[0])
        copy(es.at[block], e_out.at[block], out_sems.at[1])
        return carry

    lax.fori_loop(0, blocks, each_block, 0)
    wait_for(ys, out_sems.at[0])
    wait_for(es, out_sems.at[1])


def q_kernel(first, seqs, order, w_ref, *refs):
    row_refs, refs = refs[:seqs], refs[seqs:]
    taps_ref, q_out, x, w, fq, qs, row_sem, w_sems, out_sem = refs
    blocks = w.shape[0]
    for block in range(blocks):
        start_weights(order, w_ref, QUERY, block + first, w.at[block], w_sems.at[block])
        if block == 0:
            start_rows(row_refs, x, row_sem)
    wait_for(x, row_sem)

    def each_block(block, carry):
        wait_for(w.at[block], w_sems.at[block])
        project(x, w.at[block], fq)

        def unit(lane, s):
            qt = [wide(taps_ref[block + first, lane, pl.ds(3 * j + QUERY, 1), :]) for j in range(3)]
            qx = [fq[lane, s, t] for t in range(CHUNK + 2)]
            q = [qt[0] * qx[t + 2] + qt[1] * qx[t + 1] + qt[2] * qx[t] for t in range(CHUNK)]
            for t in range(0, CHUNK, 2):
                qs[block, lane, s, t // 2] = both(q[t], q[t + 1])

        each_unit(fq, unit)
        copy(qs.at[block], q_out.at[block], out_sem)
        return carry

    lax.fori_loop(0, blocks, each_block, 0)
    wait_for(qs, out_sem)


def gate_kernel(y_ref, e_ref, q_ref, in_ref, pole_ref, res_ref, reach_ref, out_ref, gated):
    def unit(s, carry):
        poles, states = [], []
        for n in range(0, 16, 2):
            for m, state in zip((n, n + 1), halves(e_ref[0, 0, s, n // 2])):
                pole = wide(pole_ref[0, 0, pl.ds(m, 1), :])
                state = state + reach_ref[0, 0, m] * wide(in_ref[0, 0, s, pl.ds(m, 1), :])
                poles.append(pole)
                states.append(wide(res_ref[0, 0, pl.ds(m, 1), :]) * pole * state)
        for t in range(0, CHUNK, 2):
            for u, y, q in zip((t, t + 1), halves(y_ref[0, 0, s, t // 2]), halves(q_ref[0, 0, s, t // 2])):
                total = y
                for n in range(16):
                    total += states[n]
                gated[s, pl.ds(u, 8, stride=CHUNK), :] = total * q
                states = [pole * state for pole, state in zip(poles, states)]
        return carry

    lax.fori_loop(0, gated.shape[0], unit, 0)
    out_ref[0] = gated[...].astype(BF16)


def out_kernel(seqs, order, own_ref, others_ref, w_ref, *refs):
    outs, (w, rows, sums, row_sem, w_sem, out_sems) = refs[: 2 * len(seqs)], refs[2 * len(seqs) :]
    length, channels = own_ref.shape[2:]
    half_width = w.shape[2] // 2
    for r in range(4):
        block = pl.ds(pl.multiple_of(order[r] * channels, channels), channels)
        for i, s in enumerate(seqs):
            source = own_ref.at[0, s] if r == 0 else others_ref.at[r - 1, s]
            copy(source, rows.at[pl.ds(i * length, length), block], row_sem)
    for r in range(4):
        copy(w_ref.at[r], w.at[r], w_sem)
    wait_for(rows, row_sem)
    wait_for(w, w_sem)
    for half in range(2):
        there = pl.ds(half * half_width, half_width)
        total = dot(rows[...], w[:, :, there].reshape(rows.shape[1], half_width)).astype(BF16)
        for s in range(len(seqs)):
            sums[half, s] = total[s * length : (s + 1) * length]
            copy(sums.at[half, s], outs[2 * s + half], out_sems.at[half])
    for half in range(2):
        wait_for(sums.at[half], out_sems.at[half])


def carry_states(ends, span):
    core = lax.axis_index("c")
    span = span[:, :, None]
    sent = ends.astype(BF16)
    other = from_ahead(sent, "c", 1).astype(F32)
    sent = sent.astype(F32)
    front, back = jnp.where(core == 0, sent, other), jnp.where(core == 0, other, sent)
    chip = (span * front + back).astype(BF16)
    hops = [from_behind(chip, "y", step).astype(F32) for step in (1, 2, 3)]
    square = span * span
    incoming = hops[0] + square * (hops[1] + square * hops[2])
    return jnp.where(core == 0, incoming, span * incoming + front)


IN_PLACE = pl.BlockSpec(memory_space=pl.ANY)
IN_VMEM = pl.BlockSpec(memory_space=pltpu.VMEM)
IN_SMEM = pl.BlockSpec(memory_space=pltpu.SMEM)
DMA = pltpu.SemaphoreType.DMA


def keys_values(order, w, rows, first, blocks, coefficients, name):
    seqs, (high, width) = len(rows), rows[0].shape
    lanes = coefficients[0].shape[1]
    by_chunk = (blocks, lanes, seqs, CHUNK // 2, 16, 128)
    features = pltpu.VMEM((lanes, seqs, CHUNK + 2, 8, 128), F32)
    return pl.pallas_call(
        functools.partial(kv_kernel, first, seqs),
        in_specs=[IN_SMEM] + [IN_PLACE] * (1 + seqs) + [IN_VMEM] * 4,
        out_specs=[IN_PLACE, IN_PLACE, IN_VMEM],
        scratch_shapes=[
            pltpu.VMEM((seqs * high, width), BF16),
            pltpu.VMEM((blocks, width, 2 * lanes * 128), BF16),
            features,
            features,
            pltpu.VMEM(by_chunk, BF16),
            pltpu.VMEM(by_chunk, BF16),
            DMA,
            DMA((blocks,)),
            DMA((2,)),
        ],
        out_shape=[
            jax.ShapeDtypeStruct(by_chunk, BF16),
            jax.ShapeDtypeStruct(by_chunk, BF16),
            jax.ShapeDtypeStruct((blocks, lanes, seqs, 16, 128), F32),
        ],
        compiler_params=compiler_params(),
        name=name,
    )(order, w, *rows, *coefficients)


def queries(order, w, rows, first, blocks, taps, name):
    seqs, (high, width) = len(rows), rows[0].shape
    lanes = taps.shape[1]
    by_chunk = (blocks, lanes, seqs, CHUNK // 2, 16, 128)
    return pl.pallas_call(
        functools.partial(q_kernel, first, seqs),
        in_specs=[IN_SMEM] + [IN_PLACE] * (1 + seqs) + [IN_VMEM],
        out_specs=IN_PLACE,
        scratch_shapes=[
            pltpu.VMEM((seqs * high, width), BF16),
            pltpu.VMEM((blocks, width, lanes * 128), BF16),
            pltpu.VMEM((lanes, seqs, CHUNK + 2, 8, 128), F32),
            pltpu.VMEM(by_chunk, BF16),
            DMA,
            DMA((blocks,)),
            DMA,
        ],
        out_shape=jax.ShapeDtypeStruct(by_chunk, BF16),
        compiler_params=compiler_params(),
        name=name,
    )(order, w, *rows, taps)


def gate(y, e, query, first, coefficients, name):
    blocks, lanes, seqs = y.shape[:3]
    length = CHUNK * 8
    at = lambda a, first: pl.BlockSpec((1, 1) + a.shape[2:], lambda r, lane: (r + first, lane) + (0,) * (a.ndim - 2))
    return pl.pallas_call(
        gate_kernel,
        grid=(blocks, lanes),
        in_specs=[at(a, 0) for a in (y, e, query)] + [at(a, first) for a in coefficients],
        out_specs=pl.BlockSpec((1, seqs, length, 128), lambda r, lane: (r, 0, 0, lane)),
        scratch_shapes=[pltpu.VMEM((seqs, length, 128), F32)],
        out_shape=jax.ShapeDtypeStruct((blocks, seqs, length, lanes * 128), BF16),
        compiler_params=compiler_params(),
        name=name,
    )(y, e, query, *coefficients)


def project_out(order, seqs, own, others, w, name):
    length, channels = own.shape[2:]
    blocks, half = w.shape[0], w.shape[2] // 2
    return pl.pallas_call(
        functools.partial(out_kernel, seqs),
        in_specs=[IN_SMEM] + [IN_PLACE] * 3,
        out_specs=[IN_PLACE] * (2 * len(seqs)),
        scratch_shapes=[
            pltpu.VMEM(w.shape, BF16),
            pltpu.VMEM((len(seqs) * length, blocks * channels), BF16),
            pltpu.VMEM((2, len(seqs), length, half), BF16),
            DMA,
            DMA,
            DMA((2,)),
        ],
        out_shape=[jax.ShapeDtypeStruct((length, half), BF16)] * (2 * len(seqs)),
        compiler_params=compiler_params(),
        name=name,
    )(order, own, others, w)


def shards(tokens, norm_gain, w_in, taps, decay_rate, residues, skip_gain, w_out):
    z, core = lax.axis_index("z"), lax.axis_index("c")
    part = lax.axis_index("y") * 2 + core
    width, _, channels = w_in.shape
    length = tokens.shape[1]
    blocks = seqs = len(OFFSETS)
    lanes = channels // 128
    depth = width // 8

    w_streams = w_in.transpose(1, 0, 2)
    with jax.named_scope("gather_in_weights"):
        share = lax.dynamic_slice(w_streams, (0, part * depth, 0), (3, depth, channels))
        w_all = lax.all_gather(share, ("z", "y", "c"), axis=0).reshape(blocks, 8, 3, depth, channels)

    with jax.named_scope("norm"):
        pairs = [(i, i + 1) for i in range(7)]
        edge = lax.ppermute(tokens[0, length - HEAD :], ("y", "c"), pairs)
        normed = pl.pallas_call(
            norm_kernel,
            out_shape=jax.ShapeDtypeStruct((HEAD + length, width), BF16),
            scratch_shapes=[pltpu.VMEM((width // 128, length, 128), F32)],
            compiler_params=compiler_params(),
            name="norm",
        )(edge, tokens, norm_gain[None])

    with jax.named_scope("gather_tokens"):
        rows = gather_along(normed, "x")

    with jax.named_scope("gather_out_weights"):
        w_out, normed = lax.optimization_barrier((w_out, normed))
        out_share = lax.dynamic_slice(w_out, (core * (channels // 2), 0), (channels // 2, width))
        w_o = lax.all_gather(out_share, ("z", "c"), axis=0).reshape(blocks, channels, width)

    with jax.named_scope("coefficients"):
        packed = pl.pallas_call(
            pack_kernel, out_shape=jax.ShapeDtypeStruct((48, channels), F32), name="pack"
        )(taps, decay_rate, residues, skip_gain[None])
        per_pole = jax.ShapeDtypeStruct((blocks, lanes, 16, 128), F32)
        taps_all, kern, pole, jumps, res, reach, span = pl.pallas_call(
            coefficient_kernel,
            out_shape=[
                per_pole,
                per_pole,
                per_pole,
                jax.ShapeDtypeStruct((blocks, lanes, 3, 16, 128), F32),
                per_pole,
                jax.ShapeDtypeStruct((blocks, lanes, 16, 8, 128), F32),
                per_pole,
            ],
            compiler_params=compiler_params(),
            name="coefficients",
        )(*gather_along(packed, "z"))

    order = jnp.stack([(z + step) % 4 for step in OFFSETS]).astype(jnp.int32)
    coefficients = (taps_all, kern, pole, jumps)

    y0, e0, ends0 = keys_values(order, w_streams, rows, 0, 1, coefficients, "own_keys_values")
    query0 = queries(order, w_streams, rows, 0, 1, taps_all, "own_queries")
    y0, e0, ends0, query0, w_all = lax.optimization_barrier((y0, e0, ends0, query0, w_all))

    y, e, ends = keys_values(order, w_all, rows, 1, 3, coefficients, "keys_values")
    with jax.named_scope("states"):
        incoming = carry_states(jnp.concatenate([ends0, ends], axis=0), span)
    query = queries(order, w_all, rows, 1, 3, taps_all, "queries")
    coefficients = (incoming, pole, res, reach)
    own_gated = gate(y0, e0, query0, 0, coefficients, "own_gate")
    gated = gate(y, e, query, 1, coefficients, "gate")

    far, far_b = project_out(order, (3,), own_gated, gated, w_o, "project_far")
    far, far_b, gated = lax.optimization_barrier((far, far_b, gated))
    own, own_b, near, near_b, back, back_b = project_out(order, (0, 1, 2), own_gated, gated, w_o, "project_out")

    with jax.named_scope("sum_parts"):
        passing, passing_b = from_ahead(far, "x", -1), from_ahead(far_b, "x", 1)
        direct_b, direct = from_ahead(near_b, "x", -1), from_ahead(back, "x", 1)
        added = (near.astype(F32) + passing.astype(F32)).astype(BF16)
        added_b = (back_b.astype(F32) + passing_b.astype(F32)).astype(BF16)
        added, added_b = from_ahead(added, "x", -1), from_ahead(added_b, "x", 1)
        base = tokens[0].astype(F32) + jnp.concatenate([own, own_b], axis=1).astype(F32)
        base = lax.optimization_barrier(base + jnp.concatenate([direct, direct_b], axis=1).astype(F32))
        return (base + jnp.concatenate([added, added_b], axis=1).astype(F32)).astype(BF16)[None]


def solution(mesh):
    fine = Mesh(mesh.devices.reshape(4, 4, 4, 2), ("x", "z", "y", "c"))
    fsdp, ctx = ("x", "z"), ("y", "c")
    in_specs = (
        P(fsdp, ctx, None),
        P(),
        P(None, None, fsdp),
        P(None, None, fsdp),
        P(None, fsdp),
        P(None, fsdp),
        P(fsdp),
        P(fsdp, None),
    )
    return jax.shard_map(shards, mesh=fine, in_specs=in_specs, out_specs=P(fsdp, ctx, None), check_vma=False)
```
